512 devices in a mesh: rcv: 64 (over y_lo, z, core), seg: 8 (over x, y_hi).
Axes of the slice: x: 4, y: 4 (y_hi: 2, y_lo: 2; y = y_hi * 2 + y_lo), z: 16, core: 2. Of those that a mesh axis runs over, the one named last changes fastest.
Arguments:
- traces: bfloat16 [1024, 32, 1500], P('rcv', 'seg'), may hold values from -6 to 6
- panel_start: int32 [2], replicated, may hold values from 0 to 896
- valid: int32 [32], P('seg'), may hold values 0 or 1
Outputs:
- stack: float32 [2, 128, 1024, 256], P(None, 'seg', 'rcv')
The draws below stay inside these ranges and needn't reach their ends.
All inputs are finite; a program needn't handle non-finite values. No bound on the sum of `valid` on one device may be relied on, other than what follows from the above.
Results may differ from the reference program's by a relative error of at most 0.0049.
Values may be sent and summed in bfloat16 or wider, within the bound.
A program may use at most 128 MiB of HBM per device.

```python
import math
import jax
import jax.numpy as jnp
from jax import lax

PANELS = 2
SRC = 128
SAMPLES = 1500
NFFT = 1664
K0 = 3
F = 320
LAG = 128
RCV = 1024
SEGS = 32


def place_ends(values, stream_key, low, top_value):
    longest = values.shape.index(max(values.shape))
    spots = []
    for shift in (0, 1):
        where = [jax.random.randint(jax.random.fold_in(stream_key, axis), (), 0, length) for axis, length in enumerate(values.shape)]
        where[longest] = (where[longest] + shift) % values.shape[longest]
        spots.append(tuple(where))
    return values.at[spots[0]].set(low).at[spots[1]].set(top_value)


def steps_of(key, extent, split, least, largest):
    level = 1.0
    for dim, parts in split:
        draws = jax.random.uniform(jax.random.fold_in(jax.random.fold_in(key, 6), dim), (parts,), jnp.float32, least / len(split), largest / len(split))
        level = level * jnp.repeat(jnp.exp(draws), extent[dim] // parts).reshape((-1,) + (1,) * (len(extent) - 1 - dim))
    return level


def gaussian(own_key, dims, scale, limit, split=(), kind=jnp.bfloat16):
    values = jax.random.normal(own_key, dims, jnp.float32) * scale
    if len(split) > 0:
        values = steps_of(own_key, dims, split, -0.22, 0.18) * values
    return jnp.clip(values, min=-limit, max=limit).astype(kind)


def setup_inputs(seed: int = 0) -> dict:
    seeds = jax.random.split(jax.random.key(seed), 4)
    traces = gaussian(seeds[0], (RCV, SEGS, SAMPLES), 1.0, 6.0, ((0, 64), (1, 8)))
    panel_start = jax.random.randint(seeds[1], (PANELS,), 0, RCV - SRC + 1).astype(jnp.int32)
    valid = place_ends((jax.random.randint(seeds[2], (SEGS,), 0, 4) < 3).astype(jnp.int32), jax.random.fold_in(seeds[2], 1), 0, 1)
    return dict(traces=traces, panel_start=panel_start, valid=valid)


def forward_table(samples, bins, first, length):
    times = jnp.arange(samples, dtype=jnp.int32)
    freqs = first + jnp.arange(bins, dtype=jnp.int32)
    phase = jnp.mod(times[:, None] * freqs[None, :], length).astype(jnp.float32)
    angle = 2.0 * math.pi / length * phase
    return jnp.concatenate([jnp.cos(angle), -jnp.sin(angle)], axis=1).astype(jnp.bfloat16)

def inverse_table(bins, first, length, half_lag):
    freqs = first + jnp.arange(bins, dtype=jnp.int32)
    delays = jnp.arange(2 * half_lag, dtype=jnp.int32) - half_lag
    phase = jnp.mod(freqs[:, None] * delays[None, :], length).astype(jnp.float32)
    angle = 2.0 * math.pi / length * phase
    scale = 1.0 / math.sqrt(bins)
    return jnp.concatenate([jnp.cos(angle), -jnp.sin(angle)], axis=0) * scale

def whiten(spec, bins):
    real_part = spec[:, :bins]
    imag_part = spec[:, bins:]
    power = real_part * real_part + imag_part * imag_part
    level = lax.optimization_barrier(jnp.mean(power, axis=1, keepdims=True)) + 1e-06
    factor = lax.rsqrt(power + 0.1 * level)
    return (spec * jnp.concatenate([factor, factor], axis=1)).astype(jnp.bfloat16)

def cross_lags(sources, receivers, flags, bins, inv_table, norm):
    hi = lax.Precision.HIGHEST
    src32 = sources.astype(jnp.float32) * flags[None, None, :, None]
    rcv32 = receivers.astype(jnp.float32)
    src_re, src_im = (src32[..., :bins], src32[..., bins:])
    rcv_re, rcv_im = (rcv32[..., :bins], rcv32[..., bins:])
    cross_re = jnp.einsum('psgk,bgk->psbk', src_re, rcv_re, precision=hi) + jnp.einsum('psgk,bgk->psbk', src_im, rcv_im, precision=hi)
    cross_im = jnp.einsum('psgk,bgk->psbk', src_re, rcv_im, precision=hi) - jnp.einsum('psgk,bgk->psbk', src_im, rcv_re, precision=hi)
    cross = jnp.concatenate([cross_re, cross_im], axis=3) * norm
    return jnp.einsum('psbk,kl->psbl', cross, inv_table, precision=hi)

def reference(traces, panel_start, valid):
    table = forward_table(SAMPLES, F, K0, NFFT)
    spec = jnp.dot(traces.reshape(RCV * SEGS, SAMPLES), table, preferred_element_type=jnp.float32)
    white = whiten(spec, F).reshape(RCV, SEGS, 2 * F)
    picks = panel_start[:, None].astype(jnp.int32) + jnp.arange(SRC, dtype=jnp.int32)[None, :]
    sources = white[picks]
    flags = valid.astype(jnp.float32)
    norm = 1.0 / math.sqrt(SEGS)
    inv_table = inverse_table(F, K0, NFFT, LAG)
    width = 64 if RCV % 64 == 0 else RCV
    blocks = white.reshape(RCV // width, width, SEGS, 2 * F)
    result = lax.map(lambda block: cross_lags(sources, block, flags, F, inv_table, norm), blocks)
    return jnp.transpose(result, (1, 2, 0, 3, 4)).reshape(PANELS, SRC, RCV, 2 * LAG)
```

```python
import functools
import math

import jax
import jax.numpy as jnp
import ml_dtypes
import numpy as np
from jax import lax
from jax.experimental import pallas as pl
from jax.experimental.pallas import tpu as pltpu
from jax.sharding import PartitionSpec as P

PANELS = 2
SRC = 128
NFFT = 1664
K0 = 3
F = 320
LAG = 128
SEGS = 32
Z = 16
C = 2 * F
KPAD = 1536
W = 768
MESH = pl.DeviceIdType.MESH


def column_order():
    re = np.arange(F)
    im = F + np.arange(F)
    return np.concatenate(
        [re[:128], im[:128], re[128:256], im[128:256], re[256:], im[256:]]
    )


def forward_table(samples):
    times = np.arange(samples, dtype=np.int64)
    freqs = K0 + np.arange(F, dtype=np.int64)
    phase = np.mod(times[:, None] * freqs[None, :], NFFT)
    angle = 2.0 * math.pi / NFFT * phase
    table = np.concatenate([np.cos(angle), -np.sin(angle)], axis=1)[:, column_order()]
    full = np.zeros((KPAD, C), np.float32)
    full[:samples] = table
    return full.astype(ml_dtypes.bfloat16)


def inverse_table(total_segs):
    freqs = K0 + np.arange(F, dtype=np.int64)
    delays = np.arange(2 * LAG, dtype=np.int64) - LAG
    phase = np.mod(freqs[:, None] * delays[None, :], NFFT)
    angle = 2.0 * math.pi / NFFT * phase
    scale = 1.0 / math.sqrt(F) / math.sqrt(total_segs)
    cos = np.cos(angle) * scale
    sin = np.sin(angle) * scale
    rows = [cos[:128], -sin[:128], cos[128:256], -sin[128:256]]
    rows += [cos[256:], cos[256:], -sin[256:], sin[256:]]
    return np.concatenate(rows, axis=0).astype(np.float32).astype(ml_dtypes.bfloat16)


def kernel(
    start_ref, valid_ref, tr_ref, tab_hbm, inv_hbm, out_ref,
    tab, inv, white, c1, p1, c2, src, rcv, rcvf, srcf, acc, xb,
    tab_sem, l1_send, l1_recv, l2_send, l2_recv, rc_send, rc_recv,
    ga_send, ga_recv, ring_send, ring_recv, sib_send, sib_recv,
):
    R = lax.axis_index("rcv")
    S = lax.axis_index("seg")
    yl = R // 32
    z = (R // 2) % Z
    core = R % 2
    m = R // 8
    w = R % 8
    diagonal = w == S

    def dev(yl_, z_, core_):
        return yl_ * 32 + z_ * 2 + core_

    zright = lax.rem(z + 1, Z)
    zleft = lax.rem(z + Z - 1, Z)
    sibling = dev(yl, z, 1 - core)

    tab_copies = []
    for i in range(3):
        rows = pl.ds(512 * i, 512)
        cp = pltpu.make_async_copy(tab_hbm.at[rows], tab.at[rows], tab_sem.at[i])
        cp.start()
        tab_copies.append(cp)
    inv_copy = pltpu.make_async_copy(inv_hbm, inv, tab_sem.at[3])
    inv_copy.start()

    barrier = pltpu.get_barrier_semaphore()

    def greet(r, s):
        pl.semaphore_signal(barrier, inc=1, device_id=(r, s), device_id_type=MESH)

    for d in range(1, 8):
        greet(lax.rem(m + d, 8) * 8 + w, S)
        greet(R, lax.rem(S + d, 8))
        greet(m * 8 + lax.rem(w + d, 8), w)

    @pl.when(jnp.logical_not(diagonal))
    def _():
        greet(R, w)

    for a, b in ((0, 1), (1, 0), (1, 1)):
        greet(dev(yl ^ a, z, core ^ b), S)
    greet(dev(yl, zright, core), S)
    greet(dev(yl, zleft, core), S)

    spec = None
    for i in range(3):
        tab_copies[i].wait()
        part = jnp.dot(
            tr_ref[:, pl.ds(512 * i, 512)],
            tab[pl.ds(512 * i, 512), :],
            preferred_element_type=jnp.float32,
        )
        spec = part if spec is None else spec + part
    sq = spec * spec
    pa = sq[:, 0:128] + sq[:, 128:256]
    pb = sq[:, 256:384] + sq[:, 384:512]
    pe = sq[:, 512:640]
    level = jnp.sum(pa + pb + pe, axis=1, keepdims=True) * (1.0 / F) + 1e-06
    level = 0.1 * level
    pe = pe + pltpu.roll(pe, 64, 1)
    rows = lax.broadcasted_iota(jnp.int32, (64, 1), 0) // 16
    flag = jnp.zeros((64, 1), jnp.float32)
    for g in range(4):
        flag = jnp.where(rows == g, valid_ref[g].astype(jnp.float32), flag)
    fa = lax.rsqrt(pa + level)
    fb = lax.rsqrt(pb + level)
    fe = lax.rsqrt(pe + level)
    factor = jnp.concatenate([fa, fa, fb, fb, fe], axis=1)
    whitened = (spec * factor * flag).astype(jnp.bfloat16)
    for b in range(8):
        white[b] = whitened[8 * b : 8 * b + 8]

    pl.semaphore_wait(barrier, jnp.where(diagonal, 26, 27))

    l1 = []
    for d in range(1, 8):
        other = lax.rem(m + d, 8)
        cp = pltpu.make_async_remote_copy(
            src_ref=white.at[other], dst_ref=c1.at[m],
            send_sem=l1_send.at[d], recv_sem=l1_recv.at[d],
            device_id=(other * 8 + w, S), device_id_type=MESH,
        )
        cp.start()
        l1.append(cp)
    c1[m] = white[m]

    rc = []
    for d in range(1, 8):
        cp = pltpu.make_async_remote_copy(
            src_ref=white, dst_ref=rcv.at[S],
            send_sem=rc_send.at[d], recv_sem=rc_recv.at[d],
            device_id=(R, lax.rem(S + d, 8)), device_id_type=MESH,
        )
        cp.start()
        rc.append(cp)
    rcv[S] = white[...]
    acc[...] = jnp.zeros_like(acc)

    for cp in l1:
        cp.wait_recv()
    v = lax.broadcasted_iota(jnp.int32, (8, 1), 0) + 8 * (m % 2)
    cand = [c1[mm].astype(jnp.float32) for mm in range(8)]
    for p in range(PANELS):
        st = start_ref[p]
        pick = jnp.zeros((8, C), jnp.float32)
        for mm in range(8):
            j = 128 * mm + 16 * w + v - st
            pick = jnp.where((j >= 0) & (j < SRC), cand[mm], pick)
        p1[p] = pick.astype(jnp.bfloat16)

    l2 = []
    for d in range(8):
        cp = pltpu.make_async_remote_copy(
            src_ref=p1, dst_ref=c2.at[w],
            send_sem=l2_send.at[d], recv_sem=l2_recv.at[w],
            device_id=(m * 8 + S, lax.rem(S + d, 8)), device_id_type=MESH,
        )
        l2.append(cp)
        if d == 0:
            pl.when(jnp.logical_not(diagonal))(cp.start)
        else:
            cp.start()

    @pl.when(diagonal)
    def _():
        c2[w] = p1[...]

    for ww in range(8):
        cp = pltpu.make_async_remote_copy(
            src_ref=p1, dst_ref=c2.at[ww],
            send_sem=l2_send.at[0], recv_sem=l2_recv.at[ww],
            device_id=(m * 8 + S, S), device_id_type=MESH,
        )
        pl.when(jnp.logical_not(diagonal & (w == ww)))(cp.wait_recv)

    for p in range(PANELS):
        st = start_ref[p]
        pick = jnp.zeros((8, C), jnp.float32)
        for ww in range(8):
            j = (16 * ww + v - st) & (SRC - 1)
            pick = jnp.where((j >> 4) == S, c2[ww, p].astype(jnp.float32), pick)
        src[z, yl, core, p] = pick.astype(jnp.bfloat16)

    ga = []
    for i, (a, b) in enumerate(((0, 1), (1, 0), (1, 1))):
        cp = pltpu.make_async_remote_copy(
            src_ref=src.at[z, yl, core], dst_ref=src.at[z, yl, core],
            send_sem=ga_send.at[i], recv_sem=ga_recv.at[i],
            device_id=(dev(yl ^ a, z, core ^ b), S), device_id_type=MESH,
        )
        cp.start()
        ga.append(cp)
    for cp in ga:
        cp.wait_recv()

    def ring(way, k, ref):
        return pltpu.make_async_remote_copy(
            src_ref=ref, dst_ref=ref,
            send_sem=ring_send.at[way, k], recv_sem=ring_recv.at[way, k],
            device_id=(dev(yl, zright if way == 0 else zleft, core), S),
            device_id_type=MESH,
        )

    def across(way, k, ref):
        return pltpu.make_async_remote_copy(
            src_ref=ref, dst_ref=ref,
            send_sem=sib_send.at[way, k], recv_sem=sib_recv.at[way, k],
            device_id=(sibling, S), device_id_type=MESH,
        )

    def at(way, k):
        return lax.rem(z + (Z - k if way == 0 else k), Z)

    def chunk(zc):
        zq = zc // 4
        vbase = (zq % 2) * 8
        sbase = (zc % 4) * 8 + zq // 2
        for pc in range(4):
            for p in range(PANELS):
                srcf[pc, p] = src[zc, pc // 2, pc % 2, p].astype(jnp.float32)

        def panel(p, carry):
            for vg in range(2):
                for t in range(3):
                    lanes = [pl.ds(256 * t, 128), pl.ds(256 * t + 128, 128)]
                    sums = [
                        [
                            [acc[p, vbase + vg * 4 + i, half, :, ln] for ln in lanes]
                            for half in range(2)
                        ]
                        for i in range(4)
                    ]
                    for pc in range(4):
                        seg = sbase + 4 * (pc % 2) + 2 * (pc // 2)
                        got = [
                            [rcvf[seg, half, :, ln] for ln in lanes] for half in range(2)
                        ]
                        for i in range(4):
                            row = pl.ds(vg * 4 + i, 1)
                            s0 = srcf[pc, p, row, lanes[0]]
                            if t < 2:
                                s1 = srcf[pc, p, row, lanes[1]]
                            for half in range(2):
                                r0, r1 = got[half]
                                here = sums[i][half]
                                if t < 2:
                                    here[0] = here[0] + s0 * r0 + s1 * r1
                                    here[1] = here[1] + s0 * r1 - s1 * r0
                                else:
                                    here[0] = here[0] + s0 * r0
                                    here[1] = here[1] + s0 * r1
                    for i in range(4):
                        for half in range(2):
                            for n in range(2):
                                acc[p, vbase + vg * 4 + i, half, :, lanes[n]] = sums[i][
                                    half
                                ][n]
            return carry

        lax.fori_loop(0, PANELS, panel, 0)

    for way in range(2):
        ring(way, 1, src.at[z, core]).start()

    for cp in rc:
        cp.wait_recv()

    def widen(sp, carry):
        for b in range(8):
            block = rcv[sp, b].astype(jnp.float32)
            rcvf[sp * 4 + b // 2, b % 2, :, pl.ds(0, C)] = block
            rcvf[sp * 4 + b // 2, b % 2, :, pl.ds(C, 128)] = pltpu.roll(
                block[:, 512:640], 64, 1
            )
        return carry

    lax.fori_loop(0, 8, widen, 0)
    chunk(z)

    def step(k, carry):
        for way in range(2):
            ring(way, k, src.at[at(way, k), core]).wait_recv()
        for way in range(2):
            ring(way, k + 1, src.at[at(way, k), core]).start()
        for way in range(2):
            across(way, k, src.at[at(way, k), core]).start()
        for way in range(2):
            across(way, k, src.at[at(way, k), core]).wait_recv()
        for way in range(2):
            chunk(at(way, k))
        return carry

    lax.fori_loop(1, 7, step, 0)
    last = lax.rem(z + 8, Z)
    for way in range(2):
        ring(way, 7, src.at[at(way, 7), core]).wait_recv()
    for way in range(2):
        ring(way, 8, src.at[at(way, 7), core, way]).start()
    for way in range(2):
        across(way, 7, src.at[at(way, 7), core]).start()
    for way in range(2):
        across(way, 7, src.at[at(way, 7), core]).wait_recv()
    for way in range(2):
        chunk(at(way, 7))
    for way in range(2):
        ring(way, 8, src.at[last, core, way]).wait_recv()
        across(way, 8, src.at[last, core, way]).start()
    for way in range(2):
        across(way, 8, src.at[last, core, way]).wait_recv()
    chunk(last)

    inv_copy.wait()
    for p in range(PANELS):
        st = start_ref[p]
        for i in range(16):
            xb[pl.ds(16 * i, 16)] = (
                acc[p, (st + i) & 15].reshape(16, W).astype(jnp.bfloat16)
            )
        out_ref[p] = jnp.dot(
            xb[...], inv[...], preferred_element_type=jnp.float32
        )

    for cp in l1 + rc + ga + l2[1:]:
        cp.wait_send()
    pl.when(jnp.logical_not(diagonal))(l2[0].wait_send)

    def drain(k, carry):
        for way in range(2):
            ring(way, k, src.at[z, core]).wait_send()
            across(way, k, src.at[z, core]).wait_send()
        return carry

    lax.fori_loop(1, 8, drain, 0)
    for way in range(2):
        ring(way, 8, src.at[z, core, way]).wait_send()
        across(way, 8, src.at[z, core, way]).wait_send()


def body(traces, panel_start, valid):
    rows, segs, samples = traces.shape
    table = jnp.asarray(forward_table(samples))
    inv = jnp.asarray(inverse_table(segs * lax.axis_size("seg")))
    tr = jnp.transpose(traces, (1, 0, 2)).reshape(segs * rows, samples)
    tr = jnp.pad(tr, ((0, 0), (0, KPAD - samples)))
    bf = jnp.bfloat16
    f32 = jnp.float32
    dma = pltpu.SemaphoreType.DMA
    out = pl.pallas_call(
        kernel,
        out_shape=jax.ShapeDtypeStruct((PANELS, 256, 2 * LAG), f32),
        in_specs=[
            pl.BlockSpec(memory_space=pltpu.SMEM),
            pl.BlockSpec(memory_space=pltpu.SMEM),
            pl.BlockSpec(memory_space=pltpu.VMEM),
            pl.BlockSpec(memory_space=pl.ANY),
            pl.BlockSpec(memory_space=pl.ANY),
        ],
        out_specs=pl.BlockSpec(memory_space=pltpu.VMEM),
        scratch_shapes=[
            pltpu.VMEM((KPAD, C), bf),
            pltpu.VMEM((W, 2 * LAG), bf),
            pltpu.VMEM((8, 8, C), bf),
            pltpu.VMEM((8, 8, C), bf),
            pltpu.VMEM((2, 8, C), bf),
            pltpu.VMEM((8, 2, 8, C), bf),
            pltpu.VMEM((Z, 2, 2, 2, 8, C), bf),
            pltpu.VMEM((8, 8, 8, C), bf),
            pltpu.VMEM((SEGS, 2, 8, W), f32),
            pltpu.VMEM((4, 2, 8, C), f32),
            pltpu.VMEM((2, 16, 2, 8, W), f32),
            pltpu.VMEM((256, W), bf),
            dma((4,)),
            dma((8,)), dma((8,)), dma((8,)), dma((8,)), dma((8,)), dma((8,)),
            dma((3,)), dma((3,)), dma((2, 9)), dma((2, 9)), dma((2, 9)), dma((2, 9)),
        ],
        compiler_params=pltpu.CompilerParams(
            collective_id=0, has_side_effects=True, vmem_limit_bytes=60 * 1024 * 1024
        ),
    )(panel_start, valid, tr, table, inv)
    return out.reshape(PANELS, 16, 16, 2 * LAG)


def solution(mesh):
    return jax.shard_map(
        body,
        mesh=mesh,
        in_specs=(P("rcv", "seg", None), P(), P("seg")),
        out_specs=P(None, "seg", "rcv", None),
        check_vma=False,
    )
```

```python
import functools
import math

import jax
import jax.numpy as jnp
import ml_dtypes
import numpy as np
from jax import lax
from jax.experimental import pallas as pl
from jax.experimental.pallas import tpu as pltpu
from jax.sharding import PartitionSpec as P

PANELS = 2
SRC = 128
NFFT = 1664
K0 = 3
F = 320
LAG = 128
SEGS = 32
Z = 16
C = 2 * F
KPAD = 1536
W = 768
MESH = pl.DeviceIdType.MESH


def column_order():
    re = np.arange(F)
    im = F + np.arange(F)
    return np.concatenate(
        [re[:128], im[:128], re[128:256], im[128:256], re[256:], im[256:]]
    )


def forward_table(samples):
    times = np.arange(samples, dtype=np.int64)
    freqs = K0 + np.arange(F, dtype=np.int64)
    phase = np.mod(times[:, None] * freqs[None, :], NFFT)
    angle = 2.0 * math.pi / NFFT * phase
    table = np.concatenate([np.cos(angle), -np.sin(angle)], axis=1)[:, column_order()]
    full = np.zeros((KPAD, C), np.float32)
    full[:samples] = table
    return full.astype(ml_dtypes.bfloat16)


def inverse_table(total_segs):
    freqs = K0 + np.arange(F, dtype=np.int64)
    delays = np.arange(2 * LAG, dtype=np.int64) - LAG
    phase = np.mod(freqs[:, None] * delays[None, :], NFFT)
    angle = 2.0 * math.pi / NFFT * phase
    scale = 1.0 / math.sqrt(F) / math.sqrt(total_segs)
    cos = np.cos(angle) * scale
    sin = np.sin(angle) * scale
    rows = [cos[:128], -sin[:128], cos[128:256], -sin[128:256]]
    rows += [cos[256:], cos[256:], -sin[256:], sin[256:]]
    return np.concatenate(rows, axis=0).astype(np.float32).astype(ml_dtypes.bfloat16)


def kernel(
    start_ref, valid_ref, tr_ref, tab_hbm, inv_hbm, out_ref,
    tab, inv, white, c1, p1, c2, src, rcv, rcvf, srcf, acc, xb,
    tab_sem, l1_send, l1_recv, l2_send, l2_recv, rc_send, rc_recv,
    g1_send, g1_recv, g2_send, g2_recv, sib_send, sib_recv,
):
    R = lax.axis_index("rcv")
    S = lax.axis_index("seg")
    yl = R // 32
    z = (R // 2) % Z
    core = R % 2
    m = R // 8
    w = R % 8
    zr = z % 4
    zq = z // 4
    own = w == 0

    def dev(yl_, z_, core_):
        return yl_ * 32 + z_ * 2 + core_

    def along(d):
        return lax.rem(z + Z + d, Z)

    sibling = dev(yl, z, 1 - core)

    tab_copies = []
    for i in range(3):
        rows = pl.ds(512 * i, 512)
        cp = pltpu.make_async_copy(tab_hbm.at[rows], tab.at[rows], tab_sem.at[i])
        cp.start()
        tab_copies.append(cp)
    inv_copy = pltpu.make_async_copy(inv_hbm, inv, tab_sem.at[3])
    inv_copy.start()

    barrier = pltpu.get_barrier_semaphore()

    def greet(r, s):
        pl.semaphore_signal(barrier, inc=1, device_id=(r, s), device_id_type=MESH)

    for d in range(1, 8):
        greet(lax.rem(m + d, 8) * 8 + w, S)
        greet(R, lax.rem(S + d, 8))
        greet(m * 8 + lax.rem(w + d, 8), S ^ w)

    @pl.when(jnp.logical_not(own))
    def _():
        greet(R, S ^ w)

    for d in (-2, -1, 1, 2):
        for dy in (0, 1):
            greet(dev(yl ^ dy, along(d), core), S)
    greet(sibling, S)

    samples = tr_ref.shape[1]
    spec = None
    for i in range(3):
        tab_copies[i].wait()
        part = jnp.dot(
            tr_ref[:, pl.ds(512 * i, min(512, samples - 512 * i))],
            tab[pl.ds(512 * i, min(512, samples - 512 * i)), :],
            preferred_element_type=jnp.float32,
        )
        spec = part if spec is None else spec + part
    sq = spec * spec
    pa = sq[:, 0:128] + sq[:, 128:256]
    pb = sq[:, 256:384] + sq[:, 384:512]
    pe = sq[:, 512:640]
    level = jnp.sum(pa + pb + pe, axis=1, keepdims=True) * (1.0 / F) + 1e-06
    level = 0.1 * level
    pe = pe + pltpu.roll(pe, 64, 1)
    rows = lax.broadcasted_iota(jnp.int32, (64, 1), 0) // 16
    flag = jnp.zeros((64, 1), jnp.float32)
    for g in range(4):
        flag = jnp.where(rows == g, valid_ref[g].astype(jnp.float32), flag)
    fa = lax.rsqrt(pa + level)
    fb = lax.rsqrt(pb + level)
    fe = lax.rsqrt(pe + level)
    factor = jnp.concatenate([fa, fa, fb, fb, fe], axis=1)
    whitened = (spec * factor * flag).astype(jnp.bfloat16)
    for b in range(8):
        white[b] = whitened[8 * b : 8 * b + 8]

    pl.semaphore_wait(barrier, jnp.where(own, 30, 31))

    l1 = []
    for d in range(1, 8):
        other = lax.rem(m + d, 8)
        cp = pltpu.make_async_remote_copy(
            src_ref=white.at[other], dst_ref=c1.at[m],
            send_sem=l1_send.at[d], recv_sem=l1_recv.at[d],
            device_id=(other * 8 + w, S), device_id_type=MESH,
        )
        cp.start()
        l1.append(cp)
    c1[m] = white[m]

    for cp in l1:
        cp.wait_recv()
    v = lax.broadcasted_iota(jnp.int32, (8, 1), 0) + 8 * (m % 2)
    cand = [c1[mm].astype(jnp.float32) for mm in range(8)]
    for p in range(PANELS):
        st = start_ref[p]
        pick = jnp.zeros((8, C), jnp.float32)
        for mm in range(8):
            j = 128 * mm + 16 * w + v - st
            pick = jnp.where((j >= 0) & (j < SRC), cand[mm], pick)
        p1[p] = pick.astype(jnp.bfloat16)

    l2 = []
    for d in range(8):
        to = S ^ d
        cp = pltpu.make_async_remote_copy(
            src_ref=p1, dst_ref=c2.at[w],
            send_sem=l2_send.at[d], recv_sem=l2_recv.at[w],
            device_id=(m * 8 + d, to), device_id_type=MESH,
        )
        l2.append(cp)
        if d == 0:
            pl.when(jnp.logical_not(own))(cp.start)
        else:
            cp.start()

    @pl.when(own)
    def _():
        c2[w] = p1[...]

    rc = []
    for d in range(1, 8):
        cp = pltpu.make_async_remote_copy(
            src_ref=white, dst_ref=rcv.at[S],
            send_sem=rc_send.at[d], recv_sem=rc_recv.at[d],
            device_id=(R, lax.rem(S + d, 8)), device_id_type=MESH,
        )
        cp.start()
        rc.append(cp)
    rcv[S] = white[...]
    acc[...] = jnp.zeros_like(acc)

    for ww in range(8):
        cp = pltpu.make_async_remote_copy(
            src_ref=p1, dst_ref=c2.at[ww],
            send_sem=l2_send.at[0], recv_sem=l2_recv.at[ww],
            device_id=(m * 8, S), device_id_type=MESH,
        )
        if ww == 0:
            pl.when(jnp.logical_not(own))(cp.wait_recv)
        else:
            cp.wait_recv()

    for p in range(PANELS):
        st = start_ref[p]
        pick = jnp.zeros((8, C), jnp.float32)
        for ww in range(8):
            j = (16 * ww + v - st) & (SRC - 1)
            pick = jnp.where((j >> 4) == S, c2[ww, p].astype(jnp.float32), pick)
        src[yl, core, zr, zq, p] = pick.astype(jnp.bfloat16)

    g1 = []
    for d in range(1, 4):
        piece = src.at[yl, core, zr, zq]
        cp = pltpu.make_async_remote_copy(
            src_ref=piece, dst_ref=piece,
            send_sem=g1_send.at[d], recv_sem=g1_recv.at[d],
            device_id=(dev(yl, along(4 * d), core), S), device_id_type=MESH,
        )
        cp.start()
        g1.append(cp)
    for cp in g1:
        cp.wait_recv()

    g2 = []
    for i in range(1, 8):
        dz, dy = (i // 2) ^ (i // 4), i % 2
        for half in range(2):
            to = (0, -1, 2 - 4 * half, 1)[dz]
            pair = src.at[yl, core, zr, pl.ds(2 * half, 2)]
            cp = pltpu.make_async_remote_copy(
                src_ref=pair, dst_ref=pair,
                send_sem=g2_send.at[i, half], recv_sem=g2_recv.at[i, half],
                device_id=(dev(yl ^ dy, along(to), core), S), device_id_type=MESH,
            )
            cp.start()
            g2.append(cp)

    def group(i):
        k = i // 2
        return yl ^ (i % 2), lax.rem(zr + (k ^ (k // 2)), 4)

    def across(i):
        y, q = group(i)
        four = src.at[y, core, q]
        return pltpu.make_async_remote_copy(
            src_ref=four, dst_ref=four,
            send_sem=sib_send.at[i], recv_sem=sib_recv.at[i],
            device_id=(sibling, S), device_id_type=MESH,
        )

    def chunk(i, c):
        y, q = group(i)
        sbase = 4 * ((q * 2 + c) ^ S) + 2 * y
        for n in range(4):
            for p in range(PANELS):
                srcf[n, p] = src[y, c, q, n, p].astype(jnp.float32)

        def panel(p, carry):
            for vg in range(4):
                for t in range(3):
                    lanes = [pl.ds(256 * t, 128), pl.ds(256 * t + 128, 128)]
                    sums = [
                        [
                            [acc[p, vg * 4 + i, half, :, ln] for ln in lanes]
                            for half in range(2)
                        ]
                        for i in range(4)
                    ]
                    for g in range(2):
                        n = 2 * g + vg // 2
                        got = [
                            [rcvf[sbase + g, half, :, ln] for ln in lanes]
                            for half in range(2)
                        ]
                        for i in range(4):
                            row = pl.ds((vg % 2) * 4 + i, 1)
                            s0 = srcf[n, p, row, lanes[0]]
                            if t < 2:
                                s1 = srcf[n, p, row, lanes[1]]
                            for half in range(2):
                                r0, r1 = got[half]
                                here = sums[i][half]
                                if t < 2:
                                    here[0] = here[0] + s0 * r0 + s1 * r1
                                    here[1] = here[1] + s0 * r1 - s1 * r0
                                else:
                                    here[0] = here[0] + s0 * r0
                                    here[1] = here[1] + s0 * r1
                    for i in range(4):
                        for half in range(2):
                            for n in range(2):
                                acc[p, vg * 4 + i, half, :, lanes[n]] = sums[i][half][n]
            return carry

        lax.fori_loop(0, PANELS, panel, 0)

    across(0).start()
    for cp in rc:
        cp.wait_recv()

    def widen(sp, carry):
        for b in range(8):
            block = rcv[sp, b].astype(jnp.float32)
            rcvf[sp * 4 + b // 2, b % 2, :, pl.ds(0, C)] = block
            rcvf[sp * 4 + b // 2, b % 2, :, pl.ds(C, 128)] = pltpu.roll(
                block[:, 512:640], 64, 1
            )
        return carry

    lax.fori_loop(0, 8, widen, 0)
    chunk(0, core)

    def stage(i, carry):
        for half in range(2):
            pair = src.at[yl, core, zr, pl.ds(0, 2)]
            pltpu.make_async_remote_copy(
                src_ref=pair, dst_ref=pair,
                send_sem=g2_send.at[i, half], recv_sem=g2_recv.at[i, half],
                device_id=(sibling, S), device_id_type=MESH,
            ).wait_recv()
        across(i).start()
        chunk(i, core)
        across(i - 1).wait_recv()
        chunk(i - 1, 1 - core)
        return carry

    lax.fori_loop(1, 8, stage, 0)
    across(7).wait_recv()
    chunk(7, 1 - core)

    inv_copy.wait()
    for p in range(PANELS):
        st = start_ref[p]
        for i in range(16):
            xb[pl.ds(16 * i, 16)] = (
                acc[p, (st + i) & 15].reshape(16, W).astype(jnp.bfloat16)
            )
        out_ref[p] = jnp.dot(
            xb[...], inv[...], preferred_element_type=jnp.float32
        )

    for cp in l1 + rc + g1 + g2 + l2[1:]:
        cp.wait_send()
    pl.when(jnp.logical_not(own))(l2[0].wait_send)

    def drain(i, carry):
        across(i).wait_send()
        return carry

    lax.fori_loop(0, 8, drain, 0)


def body(traces, panel_start, valid):
    rows, segs, samples = traces.shape
    table = jnp.asarray(forward_table(samples))
    inv = jnp.asarray(inverse_table(segs * lax.axis_size("seg")))
    tr = jnp.transpose(traces, (1, 0, 2)).reshape(segs * rows, samples)
    bf = jnp.bfloat16
    f32 = jnp.float32
    dma = pltpu.SemaphoreType.DMA
    out = pl.pallas_call(
        kernel,
        out_shape=jax.ShapeDtypeStruct((PANELS, 256, 2 * LAG), f32),
        in_specs=[
            pl.BlockSpec(memory_space=pltpu.SMEM),
            pl.BlockSpec(memory_space=pltpu.SMEM),
            pl.BlockSpec(memory_space=pltpu.VMEM),
            pl.BlockSpec(memory_space=pl.ANY),
            pl.BlockSpec(memory_space=pl.ANY),
        ],
        out_specs=pl.BlockSpec(memory_space=pltpu.VMEM),
        scratch_shapes=[
            pltpu.VMEM((KPAD, C), bf),
            pltpu.VMEM((W, 2 * LAG), bf),
            pltpu.VMEM((8, 8, C), bf),
            pltpu.VMEM((8, 8, C), bf),
            pltpu.VMEM((2, 8, C), bf),
            pltpu.VMEM((8, 2, 8, C), bf),
            pltpu.VMEM((2, 2, 4, 4, 2, 8, C), bf),
            pltpu.VMEM((8, 8, 8, C), bf),
            pltpu.VMEM((SEGS, 2, 8, W), f32),
            pltpu.VMEM((4, 2, 8, C), f32),
            pltpu.VMEM((2, 16, 2, 8, W), f32),
            pltpu.VMEM((256, W), bf),
            dma((4,)),
            dma((8,)), dma((8,)), dma((8,)), dma((8,)), dma((8,)), dma((8,)),
            dma((4,)), dma((4,)), dma((8, 2)), dma((8, 2)), dma((8,)), dma((8,)),
        ],
        compiler_params=pltpu.CompilerParams(
            collective_id=0, has_side_effects=True, vmem_limit_bytes=60 * 1024 * 1024
        ),
    )(panel_start, valid, tr, table, inv)
    return out.reshape(PANELS, 16, 16, 2 * LAG)


def solution(mesh):
    return jax.shard_map(
        body,
        mesh=mesh,
        in_specs=(P("rcv", "seg", None), P(), P("seg")),
        out_specs=P(None, "seg", "rcv", None),
        check_vma=False,
    )
```

```python
import functools
import math

import jax
import jax.numpy as jnp
import ml_dtypes
import numpy as np
from jax import lax
from jax.experimental import pallas as pl
from jax.experimental.pallas import tpu as pltpu
from jax.sharding import PartitionSpec as P

PANELS = 2
SRC = 128
NFFT = 1664
K0 = 3
F = 320
LAG = 128
SEGS = 32
Z = 16
C = 2 * F
KPAD = 1536
W = 768
MESH = pl.DeviceIdType.MESH


def column_order():
    re = np.arange(F)
    im = F + np.arange(F)
    return np.concatenate(
        [re[:128], im[:128], re[128:256], im[128:256], re[256:], im[256:]]
    )


def forward_table(samples):
    times = np.arange(samples, dtype=np.int64)
    freqs = K0 + np.arange(F, dtype=np.int64)
    phase = np.mod(times[:, None] * freqs[None, :], NFFT)
    angle = 2.0 * math.pi / NFFT * phase
    table = np.concatenate([np.cos(angle), -np.sin(angle)], axis=1)[:, column_order()]
    full = np.zeros((KPAD, C), np.float32)
    full[:samples] = table
    return full.astype(ml_dtypes.bfloat16)


def inverse_table(total_segs):
    freqs = K0 + np.arange(F, dtype=np.int64)
    delays = np.arange(2 * LAG, dtype=np.int64) - LAG
    phase = np.mod(freqs[:, None] * delays[None, :], NFFT)
    angle = 2.0 * math.pi / NFFT * phase
    scale = 1.0 / math.sqrt(F) / math.sqrt(total_segs)
    cos = np.cos(angle) * scale
    sin = np.sin(angle) * scale
    rows = [cos[:128], -sin[:128], cos[128:256], -sin[128:256]]
    rows += [cos[256:], cos[256:], -sin[256:], sin[256:]]
    return np.concatenate(rows, axis=0).astype(np.float32).astype(ml_dtypes.bfloat16)


def kernel(
    start_ref, valid_ref, tr_hbm, tab_hbm, out_ref,
    tr, tab, inv, white, c1, p1, c2, src, rcv, rcvf, srcf, acc, xb,
    tab_sem, l1_send, l1_recv, l2_send, l2_recv, rc_send, rc_recv,
    g1_send, g1_recv, g2_send, g2_recv, sib_send, sib_recv,
):
    R = lax.axis_index("rcv")
    S = lax.axis_index("seg")
    yl = R // 32
    z = (R // 2) % Z
    core = R % 2
    m = R // 8
    w = R % 8
    zr = z % 4
    zq = z // 4
    own = w == 0

    def dev(yl_, z_, core_):
        return yl_ * 32 + z_ * 2 + core_

    def along(d):
        return lax.rem(z + Z + d, Z)

    sibling = dev(yl, z, 1 - core)

    barrier = pltpu.get_barrier_semaphore()

    def greet(r, s):
        pl.semaphore_signal(barrier, inc=1, device_id=(r, s), device_id_type=MESH)

    for d in (2, 6, 1, 3, 5, 7, 4):
        greet(lax.rem(m + d, 8) * 8 + w, S)
    tr_copy = pltpu.make_async_copy(tr_hbm, tr, tab_sem.at[4])
    tr_copy.start()
    tab_copies = []
    for i in range(3):
        rows = pl.ds(512 * i, 512)
        cp = pltpu.make_async_copy(tab_hbm.at[rows], tab.at[rows], tab_sem.at[i])
        cp.start()
        tab_copies.append(cp)
    inv_copy = pltpu.make_async_copy(
        tab_hbm.at[pl.ds(KPAD, W), pl.ds(0, 2 * LAG)], inv, tab_sem.at[3]
    )
    inv_copy.start()
    for d in range(1, 8):
        greet(m * 8 + lax.rem(w + d, 8), S ^ w)

    @pl.when(jnp.logical_not(own))
    def _():
        greet(R, S ^ w)

    for d in (-2, -1, 1, 2):
        for dy in (0, 1):
            greet(dev(yl ^ dy, along(d), core), S)
    greet(sibling, S)
    for d in range(1, 8):
        greet(R, lax.rem(S + d, 8))

    acc[...] = jnp.zeros_like(acc)

    tr_copy.wait()
    samples = tr.shape[2]
    wide = tr[...].astype(jnp.float32)
    rows = jnp.concatenate(
        [wide[:, g, :].astype(jnp.bfloat16) for g in range(4)], axis=0
    )
    spec = None
    for i in range(3):
        tab_copies[i].wait()
        part = jnp.dot(
            rows[:, 512 * i : min(512 * i + 512, samples)],
            tab[pl.ds(512 * i, min(512, samples - 512 * i)), :],
            preferred_element_type=jnp.float32,
        )
        spec = part if spec is None else spec + part
    sq = spec * spec
    pa = sq[:, 0:128] + sq[:, 128:256]
    pb = sq[:, 256:384] + sq[:, 384:512]
    pe = sq[:, 512:640]
    level = jnp.sum(pa + pb + pe, axis=1, keepdims=True) * (1.0 / F) + 1e-06
    level = 0.1 * level
    pe = pe + pltpu.roll(pe, 64, 1)
    rows = lax.broadcasted_iota(jnp.int32, (64, 1), 0) // 16
    flag = jnp.zeros((64, 1), jnp.float32)
    for g in range(4):
        flag = jnp.where(rows == g, valid_ref[g].astype(jnp.float32), flag)
    fa = lax.rsqrt(pa + level)
    fb = lax.rsqrt(pb + level)
    fe = lax.rsqrt(pe + level)
    factor = jnp.concatenate([fa, fa, fb, fb, fe], axis=1)
    whitened = (spec * factor * flag).astype(jnp.bfloat16)
    for b in range(8):
        white[b] = whitened[8 * b : 8 * b + 8]

    pl.semaphore_wait(barrier, jnp.where(own, 30, 31))

    l1 = []
    for d in (2, 6, 1, 3, 5, 7, 4):
        other = lax.rem(m + d, 8)
        cp = pltpu.make_async_remote_copy(
            src_ref=white.at[other], dst_ref=c1.at[m],
            send_sem=l1_send.at[d], recv_sem=l1_recv.at[d],
            device_id=(other * 8 + w, S), device_id_type=MESH,
        )
        cp.start()
        l1.append(cp)
    c1[m] = white[m]

    rc = []
    for d in range(1, 8):
        cp = pltpu.make_async_remote_copy(
            src_ref=white, dst_ref=rcv.at[S],
            send_sem=rc_send.at[d], recv_sem=rc_recv.at[d],
            device_id=(R, lax.rem(S + d, 8)), device_id_type=MESH,
        )
        cp.start()
        rc.append(cp)
    rcv[S] = white[...]

    for cp in l1:
        cp.wait_recv()
    v = lax.broadcasted_iota(jnp.int32, (8, 1), 0) + 8 * (m % 2)
    cand = [c1[mm].astype(jnp.float32) for mm in range(8)]
    for p in range(PANELS):
        st = start_ref[p]
        pick = jnp.zeros((8, C), jnp.float32)
        for mm in range(8):
            j = 128 * mm + 16 * w + v - st
            pick = jnp.where((j >= 0) & (j < SRC), cand[mm], pick)
        p1[p] = pick.astype(jnp.bfloat16)

    l2 = []
    for d in range(8):
        to = S ^ d
        cp = pltpu.make_async_remote_copy(
            src_ref=p1, dst_ref=c2.at[w],
            send_sem=l2_send.at[d], recv_sem=l2_recv.at[w],
            device_id=(m * 8 + d, to), device_id_type=MESH,
        )
        l2.append(cp)
        if d == 0:
            pl.when(jnp.logical_not(own))(cp.start)
        else:
            cp.start()

    @pl.when(own)
    def _():
        c2[w] = p1[...]

    for ww in range(8):
        cp = pltpu.make_async_remote_copy(
            src_ref=p1, dst_ref=c2.at[ww],
            send_sem=l2_send.at[0], recv_sem=l2_recv.at[ww],
            device_id=(m * 8, S), device_id_type=MESH,
        )
        if ww == 0:
            pl.when(jnp.logical_not(own))(cp.wait_recv)
        else:
            cp.wait_recv()

    for p in range(PANELS):
        st = start_ref[p]
        pick = jnp.zeros((8, C), jnp.float32)
        for ww in range(8):
            j = (16 * ww + v - st) & (SRC - 1)
            pick = jnp.where((j >> 4) == S, c2[ww, p].astype(jnp.float32), pick)
        src[yl, core, zr, zq, p] = pick.astype(jnp.bfloat16)

    near = zq // 2
    far = 1 - near
    g1 = {}
    for x in (2, 1, 3):
        piece = src.at[yl, core, zr, zq]
        g1[x] = pltpu.make_async_remote_copy(
            src_ref=piece, dst_ref=piece,
            send_sem=g1_send.at[x], recv_sem=g1_recv.at[x],
            device_id=(dev(yl, (zq ^ x) * 4 + zr, core), S), device_id_type=MESH,
        )
        g1[x].start()

    def group(i):
        k = i // 2
        return yl ^ (i % 2), lax.rem(zr + (k ^ (k // 2)), 4)

    def pair(i, half, c):
        y, q = group(i)
        return src.at[y, c, q, pl.ds(2 * half, 2)]

    def window(i, half):
        dz, dy = (i // 2) ^ (i // 4), i % 2
        to = (0, -1, 2 - 4 * half, 1)[dz]
        return pltpu.make_async_remote_copy(
            src_ref=pair(0, half, core), dst_ref=pair(0, half, core),
            send_sem=g2_send.at[i, half], recv_sem=g2_recv.at[i, half],
            device_id=(dev(yl ^ dy, along(to), core), S), device_id_type=MESH,
        )

    def across(i, half):
        return pltpu.make_async_remote_copy(
            src_ref=pair(i, half, core), dst_ref=pair(i, half, core),
            send_sem=sib_send.at[i, half], recv_sem=sib_recv.at[i, half],
            device_id=(sibling, S), device_id_type=MESH,
        )

    g1[1].wait_recv()
    for i in range(1, 8):
        window(i, near).start()
    across(0, near).start()
    g1[3].wait_recv()
    g1[2].wait_recv()
    for i in range(1, 8):
        window(i, far).start()
    across(0, far).start()

    for cp in rc:
        cp.wait_recv()

    def widen(sp, carry):
        for b in range(8):
            block = rcv[sp, b].astype(jnp.float32)
            rcvf[sp * 4 + b // 2, b % 2, :, pl.ds(0, C)] = block
            rcvf[sp * 4 + b // 2, b % 2, :, pl.ds(C, 128)] = pltpu.roll(
                block[:, 512:640], 64, 1
            )
        return carry

    lax.fori_loop(0, 8, widen, 0)

    def chunk(*parts):
        segs = []
        for g, (i, half, c) in enumerate(parts):
            y, q = group(i)
            segs.append(4 * ((q * 2 + c) ^ S) + 2 * y + half)
            for n in range(2):
                for p in range(PANELS):
                    srcf[2 * g + n, p] = src[y, c, q, 2 * half + n, p].astype(
                        jnp.float32
                    )

        def panel(p, carry):
            for vg in range(4):
                for t in range(3):
                    lanes = [pl.ds(256 * t, 128), pl.ds(256 * t + 128, 128)]
                    sums = [
                        [
                            [acc[p, vg * 4 + i, half, :, ln] for ln in lanes]
                            for half in range(2)
                        ]
                        for i in range(4)
                    ]
                    for g in range(2):
                        n = 2 * g + vg // 2
                        got = [
                            [rcvf[segs[g], half, :, ln] for ln in lanes]
                            for half in range(2)
                        ]
                        for i in range(4):
                            row = pl.ds((vg % 2) * 4 + i, 1)
                            s0 = srcf[n, p, row, lanes[0]]
                            if t < 2:
                                s1 = srcf[n, p, row, lanes[1]]
                            for half in range(2):
                                r0, r1 = got[half]
                                here = sums[i][half]
                                if t < 2:
                                    here[0] = here[0] + s0 * r0 + s1 * r1
                                    here[1] = here[1] + s0 * r1 - s1 * r0
                                else:
                                    here[0] = here[0] + s0 * r0
                                    here[1] = here[1] + s0 * r1
                    for i in range(4):
                        for half in range(2):
                            for n in range(2):
                                acc[p, vg * 4 + i, half, :, lanes[n]] = sums[i][half][n]
            return carry

        lax.fori_loop(0, PANELS, panel, 0)

    def half_of(j):
        return jnp.where(j < 8, near, far)

    def arrived(i, half):
        ref = pair(0, near, core)
        return pltpu.make_async_remote_copy(
            src_ref=ref, dst_ref=ref,
            send_sem=g2_send.at[i, half], recv_sem=g2_recv.at[i, half],
            device_id=(sibling, S), device_id_type=MESH,
        )

    def take(j):
        i, half = j % 8, half_of(j)

        @pl.when(i > 0)
        def _():
            arrived(i, half).wait_recv()
            across(i, half).start()

        return i, half, core

    def given(j):
        i, half = j % 8, half_of(j)
        across(i, half).wait_recv()
        return i, half, 1 - core

    def first(t, carry):
        chunk(take(2 * t), take(2 * t + 1))
        return carry

    def middle(j, carry):
        chunk(take(j), given(j - 4))
        return carry

    def final(t, carry):
        chunk(given(2 * t), given(2 * t + 1))
        return carry

    lax.fori_loop(0, 2, first, 0)
    lax.fori_loop(4, 16, middle, 0)
    lax.fori_loop(6, 8, final, 0)

    inv_copy.wait()
    for p in range(PANELS):
        st = start_ref[p]
        for i in range(16):
            xb[pl.ds(16 * i, 16)] = (
                acc[p, (st + i) & 15].reshape(16, W).astype(jnp.bfloat16)
            )
        out_ref[p] = jnp.dot(
            xb[...], inv[...], preferred_element_type=jnp.float32
        )

    for cp in l1 + rc + [g1[1], g1[2], g1[3]] + l2[1:]:
        cp.wait_send()
    pl.when(jnp.logical_not(own))(l2[0].wait_send)

    def drain(j, carry):
        i, half = j % 8, half_of(j)
        across(i, half).wait_send()

        @pl.when(i > 0)
        def _():
            arrived(i, half).wait_send()

        return carry

    lax.fori_loop(0, 16, drain, 0)


def body(traces, panel_start, valid):
    rows, segs, samples = traces.shape
    tables = np.zeros((KPAD + W, C), ml_dtypes.bfloat16)
    tables[:KPAD] = forward_table(samples)
    tables[KPAD:, : 2 * LAG] = inverse_table(segs * lax.axis_size("seg"))
    bf = jnp.bfloat16
    f32 = jnp.float32
    dma = pltpu.SemaphoreType.DMA
    out = pl.pallas_call(
        kernel,
        out_shape=jax.ShapeDtypeStruct((PANELS, 256, 2 * LAG), f32),
        in_specs=[
            pl.BlockSpec(memory_space=pltpu.SMEM),
            pl.BlockSpec(memory_space=pltpu.SMEM),
            pl.BlockSpec(memory_space=pl.ANY),
            pl.BlockSpec(memory_space=pl.ANY),
        ],
        out_specs=pl.BlockSpec(memory_space=pltpu.VMEM),
        scratch_shapes=[
            pltpu.VMEM((rows, segs, samples), bf),
            pltpu.VMEM((KPAD, C), bf),
            pltpu.VMEM((W, 2 * LAG), bf),
            pltpu.VMEM((8, 8, C), bf),
            pltpu.VMEM((8, 8, C), bf),
            pltpu.VMEM((2, 8, C), bf),
            pltpu.VMEM((8, 2, 8, C), bf),
            pltpu.VMEM((2, 2, 4, 4, 2, 8, C), bf),
            pltpu.VMEM((8, 8, 8, C), bf),
            pltpu.VMEM((SEGS, 2, 8, W), f32),
            pltpu.VMEM((4, 2, 8, C), f32),
            pltpu.VMEM((2, 16, 2, 8, W), f32),
            pltpu.VMEM((256, W), bf),
            dma((5,)),
            dma((8,)), dma((8,)), dma((8,)), dma((8,)), dma((8,)), dma((8,)),
            dma((4,)), dma((4,)), dma((8, 2)), dma((8, 2)), dma((8, 2)), dma((8, 2)),
        ],
        compiler_params=pltpu.CompilerParams(
            collective_id=0, has_side_effects=True, vmem_limit_bytes=62 * 1024 * 1024
        ),
    )(panel_start, valid, traces, jnp.asarray(tables))
    return out.reshape(PANELS, 16, 16, 2 * LAG)


def solution(mesh):
    return jax.shard_map(
        body,
        mesh=mesh,
        in_specs=(P("rcv", "seg", None), P(), P("seg")),
        out_specs=P(None, "seg", "rcv", None),
        check_vma=False,
    )
```

```python
import functools
import math

import jax
import jax.numpy as jnp
import ml_dtypes
import numpy as np
from jax import lax
from jax.experimental import pallas as pl
from jax.experimental.pallas import tpu as pltpu
from jax.sharding import PartitionSpec as P

PANELS = 2
SRC = 128
NFFT = 1664
K0 = 3
F = 320
LAG = 128
SEGS = 32
Z = 16
C = 2 * F
KPAD = 1536
W = 768
MESH = pl.DeviceIdType.MESH


def column_order():
    re = np.arange(F)
    im = F + np.arange(F)
    return np.concatenate(
        [re[:128], im[:128], re[128:256], im[128:256], re[256:], im[256:]]
    )


def forward_table(samples):
    times = np.arange(samples, dtype=np.int64)
    freqs = K0 + np.arange(F, dtype=np.int64)
    phase = np.mod(times[:, None] * freqs[None, :], NFFT)
    angle = 2.0 * math.pi / NFFT * phase
    table = np.concatenate([np.cos(angle), -np.sin(angle)], axis=1)[:, column_order()]
    full = np.zeros((KPAD, C), np.float32)
    full[:samples] = table
    return full.astype(ml_dtypes.bfloat16)


def inverse_table():
    freqs = K0 + np.arange(F, dtype=np.int64)
    delays = np.arange(2 * LAG, dtype=np.int64) - LAG
    phase = np.mod(freqs[:, None] * delays[None, :], NFFT)
    angle = 2.0 * math.pi / NFFT * phase
    cos = np.cos(angle)
    sin = np.sin(angle)
    rows = [cos[:128], -sin[:128], cos[128:256], -sin[128:256]]
    rows += [cos[256:], cos[256:], -sin[256:], sin[256:]]
    return np.concatenate(rows, axis=0).astype(np.float32).astype(ml_dtypes.bfloat16)


def kernel(
    start_ref, valid_ref, tr_hbm, tab_hbm, out_ref,
    tr, tab, inv, white, c1, p1, c2, src, rcv, rcvf, srcf, acc, xb,
    tab_sem, l1_send, l1_recv, l2_send, l2_recv, rc_send, rc_recv,
    g1_send, g1_recv, g2_send, g2_recv, sib_send, sib_recv,
):
    R = lax.axis_index("rcv")
    S = lax.axis_index("seg")
    yl = R // 32
    z = (R // 2) % Z
    core = R % 2
    m = R // 8
    w = R % 8
    zr = z % 4
    zq = z // 4
    own = w == 0

    def dev(yl_, z_, core_):
        return yl_ * 32 + z_ * 2 + core_

    def along(d):
        return lax.rem(z + Z + d, Z)

    sibling = dev(yl, z, 1 - core)

    barrier = pltpu.get_barrier_semaphore()

    def greet(r, s):
        pl.semaphore_signal(barrier, inc=1, device_id=(r, s), device_id_type=MESH)

    for d in (2, 6, 1, 3, 5, 7, 4):
        greet(lax.rem(m + d, 8) * 8 + w, S)
    tr_copy = pltpu.make_async_copy(tr_hbm, tr, tab_sem.at[4])
    tr_copy.start()
    tab_copies = []
    for i in range(3):
        rows = pl.ds(512 * i, 512)
        cp = pltpu.make_async_copy(tab_hbm.at[rows], tab.at[rows], tab_sem.at[i])
        cp.start()
        tab_copies.append(cp)
    inv_copy = pltpu.make_async_copy(
        tab_hbm.at[pl.ds(KPAD, W), pl.ds(0, 2 * LAG)], inv, tab_sem.at[3]
    )
    inv_copy.start()
    for d in range(1, 8):
        greet(m * 8 + lax.rem(w + d, 8), S ^ w)

    @pl.when(jnp.logical_not(own))
    def _():
        greet(R, S ^ w)

    for d in (-2, -1, 1, 2):
        for dy in (0, 1):
            greet(dev(yl ^ dy, along(d), core), S)
    greet(sibling, S)
    for d in range(1, 8):
        greet(R, lax.rem(S + d, 8))

    acc[...] = jnp.zeros_like(acc)

    tr_copy.wait()
    samples = tr.shape[2]
    wide = tr[...].astype(jnp.float32)
    rows = jnp.concatenate(
        [wide[:, g, :].astype(jnp.bfloat16) for g in range(4)], axis=0
    )
    spec = None
    for i in range(3):
        tab_copies[i].wait()
        part = jnp.dot(
            rows[:, 512 * i : min(512 * i + 512, samples)],
            tab[pl.ds(512 * i, min(512, samples - 512 * i)), :],
            preferred_element_type=jnp.float32,
        )
        spec = part if spec is None else spec + part
    sq = spec * spec
    pa = sq[:, 0:128] + sq[:, 128:256]
    pb = sq[:, 256:384] + sq[:, 384:512]
    pe = sq[:, 512:640]
    level = jnp.sum(pa + pb + pe, axis=1, keepdims=True) * (1.0 / F) + 1e-06
    level = 0.1 * level
    pe = pe + pltpu.roll(pe, 64, 1)
    rows = lax.broadcasted_iota(jnp.int32, (64, 1), 0) // 16
    flag = jnp.zeros((64, 1), jnp.float32)
    for g in range(4):
        flag = jnp.where(rows == g, valid_ref[g].astype(jnp.float32), flag)
    fa = lax.rsqrt(pa + level)
    fb = lax.rsqrt(pb + level)
    fe = lax.rsqrt(pe + level)
    factor = jnp.concatenate([fa, fa, fb, fb, fe], axis=1)
    whitened = (spec * factor * flag).astype(jnp.bfloat16)
    for b in range(8):
        white[b] = whitened[8 * b : 8 * b + 8]

    pl.semaphore_wait(barrier, jnp.where(own, 30, 31))

    l1 = []
    for d in (2, 6, 1, 3, 5, 7, 4):
        other = lax.rem(m + d, 8)
        cp = pltpu.make_async_remote_copy(
            src_ref=white.at[other], dst_ref=c1.at[m],
            send_sem=l1_send.at[d], recv_sem=l1_recv.at[d],
            device_id=(other * 8 + w, S), device_id_type=MESH,
        )
        cp.start()
        l1.append(cp)
    c1[m] = white[m]

    rc = []
    for d in range(1, 8):
        cp = pltpu.make_async_remote_copy(
            src_ref=white, dst_ref=rcv.at[S],
            send_sem=rc_send.at[d], recv_sem=rc_recv.at[d],
            device_id=(R, lax.rem(S + d, 8)), device_id_type=MESH,
        )
        cp.start()
        rc.append(cp)
    rcv[S] = white[...]

    for cp in l1:
        cp.wait_recv()
    v = lax.broadcasted_iota(jnp.int32, (8, 1), 0) + 8 * (m % 2)
    cand = [c1[mm].astype(jnp.float32) for mm in range(8)]
    for p in range(PANELS):
        st = start_ref[p]
        pick = jnp.zeros((8, C), jnp.float32)
        for mm in range(8):
            j = 128 * mm + 16 * w + v - st
            pick = jnp.where((j >= 0) & (j < SRC), cand[mm], pick)
        p1[p] = pick.astype(jnp.bfloat16)

    l2 = []
    for d in range(8):
        to = S ^ d
        cp = pltpu.make_async_remote_copy(
            src_ref=p1, dst_ref=c2.at[w],
            send_sem=l2_send.at[d], recv_sem=l2_recv.at[w],
            device_id=(m * 8 + d, to), device_id_type=MESH,
        )
        l2.append(cp)
        if d == 0:
            pl.when(jnp.logical_not(own))(cp.start)
        else:
            cp.start()

    @pl.when(own)
    def _():
        c2[w] = p1[...]

    for ww in range(8):
        cp = pltpu.make_async_remote_copy(
            src_ref=p1, dst_ref=c2.at[ww],
            send_sem=l2_send.at[0], recv_sem=l2_recv.at[ww],
            device_id=(m * 8, S), device_id_type=MESH,
        )
        if ww == 0:
            pl.when(jnp.logical_not(own))(cp.wait_recv)
        else:
            cp.wait_recv()

    for p in range(PANELS):
        st = start_ref[p]
        pick = jnp.zeros((8, C), jnp.float32)
        for ww in range(8):
            j = (16 * ww + v - st) & (SRC - 1)
            pick = jnp.where((j >> 4) == S, c2[ww, p].astype(jnp.float32), pick)
        src[yl, core, zr, zq, p] = pick.astype(jnp.bfloat16)

    near = zq // 2
    far = 1 - near
    g1 = {}
    for x in (2, 1, 3):
        piece = src.at[yl, core, zr, zq]
        g1[x] = pltpu.make_async_remote_copy(
            src_ref=piece, dst_ref=piece,
            send_sem=g1_send.at[x], recv_sem=g1_recv.at[x],
            device_id=(dev(yl, (zq ^ x) * 4 + zr, core), S), device_id_type=MESH,
        )
        g1[x].start()

    def group(i):
        k = i // 2
        return yl ^ (i % 2), lax.rem(zr + (k ^ (k // 2)), 4)

    def pair(i, half, c):
        y, q = group(i)
        return src.at[y, c, q, pl.ds(2 * half, 2)]

    def window(i, half):
        dz, dy = (i // 2) ^ (i // 4), i % 2
        to = (0, -1, 2 - 4 * half, 1)[dz]
        return pltpu.make_async_remote_copy(
            src_ref=pair(0, half, core), dst_ref=pair(0, half, core),
            send_sem=g2_send.at[i, half], recv_sem=g2_recv.at[i, half],
            device_id=(dev(yl ^ dy, along(to), core), S), device_id_type=MESH,
        )

    def across(i, half):
        return pltpu.make_async_remote_copy(
            src_ref=pair(i, half, core), dst_ref=pair(i, half, core),
            send_sem=sib_send.at[i, half], recv_sem=sib_recv.at[i, half],
            device_id=(sibling, S), device_id_type=MESH,
        )

    g1[1].wait_recv()
    for i in range(1, 8):
        window(i, near).start()
    across(0, near).start()
    g1[3].wait_recv()
    g1[2].wait_recv()
    for i in range(1, 8):
        window(i, far).start()
    across(0, far).start()

    for cp in rc:
        cp.wait_recv()

    def widen(sp, carry):
        for b in range(8):
            block = rcv[sp, b].astype(jnp.float32)
            rcvf[sp * 4 + b // 2, b % 2, :, pl.ds(0, C)] = block
            rcvf[sp * 4 + b // 2, b % 2, :, pl.ds(C, 128)] = pltpu.roll(
                block[:, 512:640], 64, 1
            )
        return carry

    lax.fori_loop(0, 8, widen, 0)

    def chunk(*parts):
        segs = []
        for g, (i, half, c) in enumerate(parts):
            y, q = group(i)
            segs.append(4 * ((q * 2 + c) ^ S) + 2 * y + half)
            for n in range(2):
                for p in range(PANELS):
                    srcf[2 * g + n, p] = src[y, c, q, 2 * half + n, p].astype(
                        jnp.float32
                    )

        def panel(p, carry):
            for vg in range(4):
                for t in range(3):
                    lanes = [pl.ds(256 * t, 128), pl.ds(256 * t + 128, 128)]
                    sums = [
                        [
                            [acc[p, vg * 4 + i, half, :, ln] for ln in lanes]
                            for half in range(2)
                        ]
                        for i in range(4)
                    ]
                    for g in range(2):
                        n = 2 * g + vg // 2
                        got = [
                            [rcvf[segs[g], half, :, ln] for ln in lanes]
                            for half in range(2)
                        ]
                        for i in range(4):
                            row = pl.ds((vg % 2) * 4 + i, 1)
                            s0 = srcf[n, p, row, lanes[0]]
                            if t < 2:
                                s1 = srcf[n, p, row, lanes[1]]
                            for half in range(2):
                                r0, r1 = got[half]
                                here = sums[i][half]
                                if t < 2:
                                    here[0] = here[0] + s0 * r0 + s1 * r1
                                    here[1] = here[1] + s0 * r1 - s1 * r0
                                else:
                                    here[0] = here[0] + s0 * r0
                                    here[1] = here[1] + s0 * r1
                    for i in range(4):
                        for half in range(2):
                            for n in range(2):
                                acc[p, vg * 4 + i, half, :, lanes[n]] = sums[i][half][n]
            return carry

        lax.fori_loop(0, PANELS, panel, 0)

    def half_of(j):
        return jnp.where(j < 8, near, far)

    def arrived(i, half):
        ref = pair(0, near, core)
        return pltpu.make_async_remote_copy(
            src_ref=ref, dst_ref=ref,
            send_sem=g2_send.at[i, half], recv_sem=g2_recv.at[i, half],
            device_id=(sibling, S), device_id_type=MESH,
        )

    def take(j):
        i, half = j % 8, half_of(j)

        @pl.when(i > 0)
        def _():
            arrived(i, half).wait_recv()
            across(i, half).start()

        return i, half, core

    def given(j):
        i, half = j % 8, half_of(j)
        across(i, half).wait_recv()
        return i, half, 1 - core

    def first(t, carry):
        chunk(take(2 * t), take(2 * t + 1))
        return carry

    def middle(j, carry):
        chunk(take(j), given(j - 4))
        return carry

    def final(t, carry):
        chunk(given(2 * t), given(2 * t + 1))
        return carry

    lax.fori_loop(0, 2, first, 0)
    lax.fori_loop(4, 16, middle, 0)
    lax.fori_loop(6, 8, final, 0)

    inv_copy.wait()
    for p in range(PANELS):
        st = start_ref[p]
        for i in range(16):
            xb[pl.ds(16 * i, 16)] = (
                acc[p, (st + i) & 15].reshape(16, W).astype(jnp.bfloat16)
            )
        out_ref[p] = jnp.dot(
            xb[...], inv[...], preferred_element_type=jnp.float32
        )

    for cp in l1 + rc + [g1[1], g1[2], g1[3]] + l2[1:]:
        cp.wait_send()
    pl.when(jnp.logical_not(own))(l2[0].wait_send)

    def drain(j, carry):
        i, half = j % 8, half_of(j)
        across(i, half).wait_send()

        @pl.when(i > 0)
        def _():
            arrived(i, half).wait_send()

        return carry

    lax.fori_loop(0, 16, drain, 0)


def body(traces, panel_start, valid):
    rows, segs, samples = traces.shape
    tables = np.zeros((KPAD + W, C), ml_dtypes.bfloat16)
    tables[:KPAD] = forward_table(samples)
    tables[KPAD:, : 2 * LAG] = inverse_table()
    bf = jnp.bfloat16
    f32 = jnp.float32
    dma = pltpu.SemaphoreType.DMA
    out = pl.pallas_call(
        kernel,
        out_shape=jax.ShapeDtypeStruct((PANELS, 256, 2 * LAG), f32),
        in_specs=[
            pl.BlockSpec(memory_space=pltpu.SMEM),
            pl.BlockSpec(memory_space=pltpu.SMEM),
            pl.BlockSpec(memory_space=pl.ANY),
            pl.BlockSpec(memory_space=pl.ANY),
        ],
        out_specs=pl.BlockSpec(memory_space=pltpu.VMEM),
        scratch_shapes=[
            pltpu.VMEM((rows, segs, samples), bf),
            pltpu.VMEM((KPAD, C), bf),
            pltpu.VMEM((W, 2 * LAG), bf),
            pltpu.VMEM((8, 8, C), bf),
            pltpu.VMEM((8, 8, C), bf),
            pltpu.VMEM((2, 8, C), bf),
            pltpu.VMEM((8, 2, 8, C), bf),
            pltpu.VMEM((2, 2, 4, 4, 2, 8, C), bf),
            pltpu.VMEM((8, 8, 8, C), bf),
            pltpu.VMEM((SEGS, 2, 8, W), f32),
            pltpu.VMEM((4, 2, 8, C), f32),
            pltpu.VMEM((2, 16, 2, 8, W), f32),
            pltpu.VMEM((256, W), bf),
            dma((5,)),
            dma((8,)), dma((8,)), dma((8,)), dma((8,)), dma((8,)), dma((8,)),
            dma((4,)), dma((4,)), dma((8, 2)), dma((8, 2)), dma((8, 2)), dma((8, 2)),
        ],
        compiler_params=pltpu.CompilerParams(
            collective_id=0, has_side_effects=True, vmem_limit_bytes=62 * 1024 * 1024
        ),
    )(panel_start, valid, traces, jnp.asarray(tables))
    total_segs = segs * lax.axis_size("seg")
    out = out * (1.0 / math.sqrt(F * total_segs))
    return out.reshape(PANELS, 16, 16, 2 * LAG)


def solution(mesh):
    return jax.shard_map(
        body,
        mesh=mesh,
        in_specs=(P("rcv", "seg", None), P(), P("seg")),
        out_specs=P(None, "seg", "rcv", None),
        check_vma=False,
    )
```

```python
import functools
import math

import jax
import jax.numpy as jnp
import ml_dtypes
import numpy as np
from jax import lax
from jax.experimental import pallas as pl
from jax.experimental.pallas import tpu as pltpu
from jax.sharding import PartitionSpec as P

PANELS = 2
SRC = 128
NFFT = 1664
K0 = 3
F = 320
LAG = 128
SEGS = 32
Z = 16
C = 2 * F
KPAD = 1536
W = 768
MESH = pl.DeviceIdType.MESH


def column_order():
    re = np.arange(F)
    im = F + np.arange(F)
    return np.concatenate(
        [re[:128], im[:128], re[128:256], im[128:256], re[256:], im[256:]]
    )


def forward_table(samples):
    times = np.arange(samples, dtype=np.int64)
    freqs = K0 + np.arange(F, dtype=np.int64)
    phase = np.mod(times[:, None] * freqs[None, :], NFFT)
    angle = 2.0 * math.pi / NFFT * phase
    table = np.concatenate([np.cos(angle), -np.sin(angle)], axis=1)[:, column_order()]
    full = np.zeros((KPAD, C), np.float32)
    full[:samples] = table
    return full.astype(ml_dtypes.bfloat16)


def inverse_table():
    freqs = K0 + np.arange(F, dtype=np.int64)
    delays = np.arange(2 * LAG, dtype=np.int64) - LAG
    phase = np.mod(freqs[:, None] * delays[None, :], NFFT)
    angle = 2.0 * math.pi / NFFT * phase
    cos = np.cos(angle)
    sin = np.sin(angle)
    rows = [cos[:128], -sin[:128], cos[128:256], -sin[128:256]]
    rows += [cos[256:], cos[256:], -sin[256:], sin[256:]]
    return np.concatenate(rows, axis=0).astype(np.float32).astype(ml_dtypes.bfloat16)


def kernel(
    start_ref, valid_ref, tr_hbm, tab_hbm, out_ref,
    tr, tab, inv, white, c1, p1, c2, src, rcv, rcvf, srcf, acc, xb,
    tab_sem, l1_send, l1_recv, l2_send, l2_recv, rc_send, rc_recv,
    g1_send, g1_recv, g2_send, g2_recv, sib_send, sib_recv,
):
    R = lax.axis_index("rcv")
    S = lax.axis_index("seg")
    yl = R // 32
    z = (R // 2) % Z
    core = R % 2
    m = R // 8
    w = R % 8
    zr = z % 4
    zq = z // 4
    own = w == 0

    def dev(yl_, z_, core_):
        return yl_ * 32 + z_ * 2 + core_

    def along(d):
        return lax.rem(z + Z + d, Z)

    sibling = dev(yl, z, 1 - core)

    barrier = pltpu.get_barrier_semaphore()

    def greet(r, s):
        pl.semaphore_signal(barrier, inc=1, device_id=(r, s), device_id_type=MESH)

    for d in (2, 6, 1, 3, 5, 7, 4):
        greet(lax.rem(m + d, 8) * 8 + w, S)
    tr_copy = pltpu.make_async_copy(tr_hbm, tr, tab_sem.at[4])
    tr_copy.start()
    tab_copies = []
    for i in range(3):
        rows = pl.ds(512 * i, 512)
        cp = pltpu.make_async_copy(tab_hbm.at[rows], tab.at[rows], tab_sem.at[i])
        cp.start()
        tab_copies.append(cp)
    inv_copy = pltpu.make_async_copy(
        tab_hbm.at[pl.ds(KPAD, W), pl.ds(0, 2 * LAG)], inv, tab_sem.at[3]
    )
    inv_copy.start()
    for d in range(1, 8):
        greet(m * 8 + lax.rem(w + d, 8), S ^ w)

    @pl.when(jnp.logical_not(own))
    def _():
        greet(R, S ^ w)

    for d in (-2, -1, 1, 2):
        for dy in (0, 1):
            greet(dev(yl ^ dy, along(d), core), S)
    greet(sibling, S)
    for d in range(1, 8):
        greet(R, lax.rem(S + d, 8))

    acc[...] = jnp.zeros_like(acc)

    tr_copy.wait()
    samples = tr.shape[2]
    wide = tr[...].astype(jnp.float32)
    rows = jnp.concatenate(
        [wide[:, g, :].astype(jnp.bfloat16) for g in range(4)], axis=0
    )
    spec = None
    for i in range(3):
        tab_copies[i].wait()
        part = jnp.dot(
            rows[:, 512 * i : min(512 * i + 512, samples)],
            tab[pl.ds(512 * i, min(512, samples - 512 * i)), :],
            preferred_element_type=jnp.float32,
        )
        spec = part if spec is None else spec + part
    sq = spec * spec
    pa = sq[:, 0:128] + sq[:, 128:256]
    pb = sq[:, 256:384] + sq[:, 384:512]
    pe = sq[:, 512:640]
    level = jnp.sum(pa + pb + pe, axis=1, keepdims=True) * (1.0 / F) + 1e-06
    level = 0.1 * level
    pe = pe + pltpu.roll(pe, 64, 1)
    rows = lax.broadcasted_iota(jnp.int32, (64, 1), 0) // 16
    flag = jnp.zeros((64, 1), jnp.float32)
    for g in range(4):
        flag = jnp.where(rows == g, valid_ref[g].astype(jnp.float32), flag)
    fa = lax.rsqrt(pa + level)
    fb = lax.rsqrt(pb + level)
    fe = lax.rsqrt(pe + level)
    factor = jnp.concatenate([fa, fa, fb, fb, fe], axis=1)
    whitened = (spec * factor * flag).astype(jnp.bfloat16)
    for b in range(8):
        white[b] = whitened[8 * b : 8 * b + 8]

    pl.semaphore_wait(barrier, jnp.where(own, 30, 31))

    l1 = []
    for d in (2, 6, 1, 3, 5, 7, 4):
        other = lax.rem(m + d, 8)
        cp = pltpu.make_async_remote_copy(
            src_ref=white.at[other], dst_ref=c1.at[m],
            send_sem=l1_send.at[d], recv_sem=l1_recv.at[d],
            device_id=(other * 8 + w, S), device_id_type=MESH,
        )
        cp.start()
        l1.append(cp)
    c1[m] = white[m]

    rc = []
    for d in range(1, 8):
        cp = pltpu.make_async_remote_copy(
            src_ref=white, dst_ref=rcv.at[S],
            send_sem=rc_send.at[d], recv_sem=rc_recv.at[d],
            device_id=(R, lax.rem(S + d, 8)), device_id_type=MESH,
        )
        cp.start()
        rc.append(cp)
    rcv[S] = white[...]

    for cp in l1:
        cp.wait_recv()
    v = lax.broadcasted_iota(jnp.int32, (8, 1), 0) + 8 * (m % 2)
    cand = [c1[mm].astype(jnp.float32) for mm in range(8)]
    for p in range(PANELS):
        st = start_ref[p]
        pick = jnp.zeros((8, C), jnp.float32)
        for mm in range(8):
            j = 128 * mm + 16 * w + v - st
            pick = jnp.where((j >= 0) & (j < SRC), cand[mm], pick)
        p1[p] = pick.astype(jnp.bfloat16)

    l2 = []
    for d in range(8):
        to = S ^ d
        cp = pltpu.make_async_remote_copy(
            src_ref=p1, dst_ref=c2.at[w],
            send_sem=l2_send.at[d], recv_sem=l2_recv.at[w],
            device_id=(m * 8 + d, to), device_id_type=MESH,
        )
        l2.append(cp)
        if d == 0:
            pl.when(jnp.logical_not(own))(cp.start)
        else:
            cp.start()

    @pl.when(own)
    def _():
        c2[w] = p1[...]

    for ww in range(8):
        cp = pltpu.make_async_remote_copy(
            src_ref=p1, dst_ref=c2.at[ww],
            send_sem=l2_send.at[0], recv_sem=l2_recv.at[ww],
            device_id=(m * 8, S), device_id_type=MESH,
        )
        if ww == 0:
            pl.when(jnp.logical_not(own))(cp.wait_recv)
        else:
            cp.wait_recv()

    for p in range(PANELS):
        st = start_ref[p]
        pick = jnp.zeros((8, C), jnp.float32)
        for ww in range(8):
            j = (16 * ww + v - st) & (SRC - 1)
            pick = jnp.where((j >> 4) == S, c2[ww, p].astype(jnp.float32), pick)
        src[yl, core, zr, zq, p] = pick.astype(jnp.bfloat16)

    near = zq // 2
    far = 1 - near
    g1 = {}
    for x in (2, 1, 3):
        piece = src.at[yl, core, zr, zq]
        g1[x] = pltpu.make_async_remote_copy(
            src_ref=piece, dst_ref=piece,
            send_sem=g1_send.at[x], recv_sem=g1_recv.at[x],
            device_id=(dev(yl, (zq ^ x) * 4 + zr, core), S), device_id_type=MESH,
        )
        g1[x].start()

    def group(i):
        k = i // 2
        return yl ^ (i % 2), lax.rem(zr + (k ^ (k // 2)), 4)

    def pair(i, half, c):
        y, q = group(i)
        return src.at[y, c, q, pl.ds(2 * half, 2)]

    def window(i, half, ref):
        dz, dy = (i // 2) ^ (i // 4), i % 2
        to = (0, -1, 2 - 4 * half, 1)[dz]
        return pltpu.make_async_remote_copy(
            src_ref=ref, dst_ref=ref,
            send_sem=g2_send.at[i, half], recv_sem=g2_recv.at[i, half],
            device_id=(dev(yl ^ dy, along(to), core), S), device_id_type=MESH,
        )

    def across(i, half):
        return pltpu.make_async_remote_copy(
            src_ref=pair(i, half, core), dst_ref=pair(i, half, core),
            send_sem=sib_send.at[i, half], recv_sem=sib_recv.at[i, half],
            device_id=(sibling, S), device_id_type=MESH,
        )

    for i in range(1, 8):
        window(i, near, src.at[yl, core, zr, zq]).start()
    g1[1].wait_recv()
    for i in range(1, 8):
        window(i, near, src.at[yl, core, zr, zq ^ 1]).start()
    across(0, near).start()
    g1[3].wait_recv()
    g1[2].wait_recv()
    for i in range(1, 8):
        window(i, far, pair(0, far, core)).start()
    across(0, far).start()

    for cp in rc:
        cp.wait_recv()

    def widen(sp, carry):
        for b in range(8):
            block = rcv[sp, b].astype(jnp.float32)
            rcvf[sp * 4 + b // 2, b % 2, :, pl.ds(0, C)] = block
            rcvf[sp * 4 + b // 2, b % 2, :, pl.ds(C, 128)] = pltpu.roll(
                block[:, 512:640], 64, 1
            )
        return carry

    lax.fori_loop(0, 8, widen, 0)

    def chunk(*parts):
        segs = []
        for g, (i, half, c) in enumerate(parts):
            y, q = group(i)
            segs.append(4 * ((q * 2 + c) ^ S) + 2 * y + half)
            for n in range(2):
                for p in range(PANELS):
                    srcf[2 * g + n, p] = src[y, c, q, 2 * half + n, p].astype(
                        jnp.float32
                    )

        def panel(p, carry):
            for vg in range(4):
                for t in range(3):
                    lanes = [pl.ds(256 * t, 128), pl.ds(256 * t + 128, 128)]
                    sums = [
                        [
                            [acc[p, vg * 4 + i, half, :, ln] for ln in lanes]
                            for half in range(2)
                        ]
                        for i in range(4)
                    ]
                    for g in range(2):
                        n = 2 * g + vg // 2
                        got = [
                            [rcvf[segs[g], half, :, ln] for ln in lanes]
                            for half in range(2)
                        ]
                        for i in range(4):
                            row = pl.ds((vg % 2) * 4 + i, 1)
                            s0 = srcf[n, p, row, lanes[0]]
                            if t < 2:
                                s1 = srcf[n, p, row, lanes[1]]
                            for half in range(2):
                                r0, r1 = got[half]
                                here = sums[i][half]
                                if t < 2:
                                    here[0] = here[0] + s0 * r0 + s1 * r1
                                    here[1] = here[1] + s0 * r1 - s1 * r0
                                else:
                                    here[0] = here[0] + s0 * r0
                                    here[1] = here[1] + s0 * r1
                    for i in range(4):
                        for half in range(2):
                            for n in range(2):
                                acc[p, vg * 4 + i, half, :, lanes[n]] = sums[i][half][n]
            return carry

        lax.fori_loop(0, PANELS, panel, 0)

    def half_of(j):
        return jnp.where(j < 8, near, far)

    def arrived(i, half):
        ref = pair(0, near, core)
        return pltpu.make_async_remote_copy(
            src_ref=ref, dst_ref=ref,
            send_sem=g2_send.at[i, half], recv_sem=g2_recv.at[i, half],
            device_id=(sibling, S), device_id_type=MESH,
        )

    def take(j):
        i, half = j % 8, half_of(j)

        @pl.when(i > 0)
        def _():
            arrived(i, half).wait_recv()
            across(i, half).start()

        return i, half, core

    def given(j):
        i, half = j % 8, half_of(j)
        across(i, half).wait_recv()
        return i, half, 1 - core

    def first(t, carry):
        chunk(take(2 * t), take(2 * t + 1))
        return carry

    def middle(j, carry):
        chunk(take(j), given(j - 4))
        return carry

    def final(t, carry):
        chunk(given(2 * t), given(2 * t + 1))
        return carry

    lax.fori_loop(0, 2, first, 0)
    lax.fori_loop(4, 16, middle, 0)
    lax.fori_loop(6, 8, final, 0)

    inv_copy.wait()
    for p in range(PANELS):
        st = start_ref[p]
        for i in range(16):
            xb[pl.ds(16 * i, 16)] = (
                acc[p, (st + i) & 15].reshape(16, W).astype(jnp.bfloat16)
            )
        out_ref[p] = jnp.dot(
            xb[...], inv[...], preferred_element_type=jnp.float32
        )

    for cp in l1 + rc + [g1[1], g1[2], g1[3]] + l2[1:]:
        cp.wait_send()
    pl.when(jnp.logical_not(own))(l2[0].wait_send)

    def drain(j, carry):
        i, half = j % 8, half_of(j)
        across(i, half).wait_send()

        @pl.when(i > 0)
        def _():
            arrived(i, half).wait_send()

        return carry

    lax.fori_loop(0, 16, drain, 0)


def body(traces, panel_start, valid):
    rows, segs, samples = traces.shape
    tables = np.zeros((KPAD + W, C), ml_dtypes.bfloat16)
    tables[:KPAD] = forward_table(samples)
    tables[KPAD:, : 2 * LAG] = inverse_table()
    bf = jnp.bfloat16
    f32 = jnp.float32
    dma = pltpu.SemaphoreType.DMA
    out = pl.pallas_call(
        kernel,
        out_shape=jax.ShapeDtypeStruct((PANELS, 256, 2 * LAG), f32),
        in_specs=[
            pl.BlockSpec(memory_space=pltpu.SMEM),
            pl.BlockSpec(memory_space=pltpu.SMEM),
            pl.BlockSpec(memory_space=pl.ANY),
            pl.BlockSpec(memory_space=pl.ANY),
        ],
        out_specs=pl.BlockSpec(memory_space=pltpu.VMEM),
        scratch_shapes=[
            pltpu.VMEM((rows, segs, samples), bf),
            pltpu.VMEM((KPAD, C), bf),
            pltpu.VMEM((W, 2 * LAG), bf),
            pltpu.VMEM((8, 8, C), bf),
            pltpu.VMEM((8, 8, C), bf),
            pltpu.VMEM((2, 8, C), bf),
            pltpu.VMEM((8, 2, 8, C), bf),
            pltpu.VMEM((2, 2, 4, 4, 2, 8, C), bf),
            pltpu.VMEM((8, 8, 8, C), bf),
            pltpu.VMEM((SEGS, 2, 8, W), f32),
            pltpu.VMEM((4, 2, 8, C), f32),
            pltpu.VMEM((2, 16, 2, 8, W), f32),
            pltpu.VMEM((256, W), bf),
            dma((5,)),
            dma((8,)), dma((8,)), dma((8,)), dma((8,)), dma((8,)), dma((8,)),
            dma((4,)), dma((4,)), dma((8, 2)), dma((8, 2)), dma((8, 2)), dma((8, 2)),
        ],
        compiler_params=pltpu.CompilerParams(
            collective_id=0, has_side_effects=True, vmem_limit_bytes=62 * 1024 * 1024
        ),
    )(panel_start, valid, traces, jnp.asarray(tables))
    total_segs = segs * lax.axis_size("seg")
    out = out * (1.0 / math.sqrt(F * total_segs))
    return out.reshape(PANELS, 16, 16, 2 * LAG)


def solution(mesh):
    return jax.shard_map(
        body,
        mesh=mesh,
        in_specs=(P("rcv", "seg", None), P(), P("seg")),
        out_specs=P(None, "seg", "rcv", None),
        check_vma=False,
    )
```

```python
import functools
import math

import jax
import jax.numpy as jnp
import ml_dtypes
import numpy as np
from jax import lax
from jax.experimental import pallas as pl
from jax.experimental.pallas import tpu as pltpu
from jax.sharding import PartitionSpec as P

PANELS = 2
SRC = 128
NFFT = 1664
K0 = 3
F = 320
LAG = 128
SEGS = 32
Z = 16
C = 2 * F
KPAD = 1536
W = 768
MESH = pl.DeviceIdType.MESH


def column_order():
    re = np.arange(F)
    im = F + np.arange(F)
    return np.concatenate(
        [re[:128], im[:128], re[128:256], im[128:256], re[256:], im[256:]]
    )


def forward_table(samples):
    times = np.arange(samples, dtype=np.int64)
    freqs = K0 + np.arange(F, dtype=np.int64)
    phase = np.mod(times[:, None] * freqs[None, :], NFFT)
    angle = 2.0 * math.pi / NFFT * phase
    table = np.concatenate([np.cos(angle), -np.sin(angle)], axis=1)[:, column_order()]
    full = np.zeros((KPAD, C), np.float32)
    full[:samples] = table
    return full.astype(ml_dtypes.bfloat16)


def inverse_table():
    freqs = K0 + np.arange(F, dtype=np.int64)
    delays = np.arange(2 * LAG, dtype=np.int64) - LAG
    phase = np.mod(freqs[:, None] * delays[None, :], NFFT)
    angle = 2.0 * math.pi / NFFT * phase
    cos = np.cos(angle)
    sin = np.sin(angle)
    rows = [cos[:128], -sin[:128], cos[128:256], -sin[128:256]]
    rows += [cos[256:], cos[256:], -sin[256:], sin[256:]]
    return np.concatenate(rows, axis=0).astype(np.float32).astype(ml_dtypes.bfloat16)


def kernel(
    start_ref, valid_ref, tr_hbm, tab_hbm, out_ref,
    tr, tab, inv, white, c1, p1, c2, src, rcv, rcvf, srcf, acc, xb,
    tab_sem, l1_send, l1_recv, l2_send, l2_recv, rc_send, rc_recv,
    g1_send, g1_recv, g2_send, g2_recv, sib_send, sib_recv,
):
    R = lax.axis_index("rcv")
    S = lax.axis_index("seg")
    yl = R // 32
    z = (R // 2) % Z
    core = R % 2
    m = R // 8
    w = R % 8
    zr = z % 4
    zq = z // 4
    own = w == 0

    def dev(yl_, z_, core_):
        return yl_ * 32 + z_ * 2 + core_

    def along(d):
        return lax.rem(z + Z + d, Z)

    sibling = dev(yl, z, 1 - core)

    barrier = pltpu.get_barrier_semaphore()

    def greet(r, s):
        pl.semaphore_signal(barrier, inc=1, device_id=(r, s), device_id_type=MESH)

    for d in (2, 6, 1, 3, 5, 7, 4):
        greet(lax.rem(m + d, 8) * 8 + w, S)
    tr_copy = pltpu.make_async_copy(tr_hbm, tr, tab_sem.at[4])
    tr_copy.start()
    tab_copies = []
    for i in range(3):
        rows = pl.ds(512 * i, 512)
        cp = pltpu.make_async_copy(tab_hbm.at[rows], tab.at[rows], tab_sem.at[i])
        cp.start()
        tab_copies.append(cp)
    inv_copy = pltpu.make_async_copy(
        tab_hbm.at[pl.ds(KPAD, W), pl.ds(0, 2 * LAG)], inv, tab_sem.at[3]
    )
    inv_copy.start()
    for d in range(1, 8):
        greet(m * 8 + lax.rem(w + d, 8), S ^ w)

    @pl.when(jnp.logical_not(own))
    def _():
        greet(R, S ^ w)

    for d in (-2, -1, 1, 2):
        for dy in (0, 1):
            greet(dev(yl ^ dy, along(d), core), S)
    greet(sibling, S)
    for d in range(1, 8):
        greet(R, lax.rem(S + d, 8))

    acc[...] = jnp.zeros_like(acc)

    tr_copy.wait()
    samples = tr.shape[2]
    wide = tr[...].astype(jnp.float32)
    rows = jnp.concatenate(
        [wide[:, g, :].astype(jnp.bfloat16) for g in range(4)], axis=0
    )
    spec = None
    for i in range(3):
        tab_copies[i].wait()
        part = jnp.dot(
            rows[:, 512 * i : min(512 * i + 512, samples)],
            tab[pl.ds(512 * i, min(512, samples - 512 * i)), :],
            preferred_element_type=jnp.float32,
        )
        spec = part if spec is None else spec + part
    sq = spec * spec
    pa = sq[:, 0:128] + sq[:, 128:256]
    pb = sq[:, 256:384] + sq[:, 384:512]
    pe = sq[:, 512:640]
    level = jnp.sum(pa + pb + pe, axis=1, keepdims=True) * (1.0 / F) + 1e-06
    level = 0.1 * level
    pe = pe + pltpu.roll(pe, 64, 1)
    rows = lax.broadcasted_iota(jnp.int32, (64, 1), 0) // 16
    flag = jnp.zeros((64, 1), jnp.float32)
    for g in range(4):
        flag = jnp.where(rows == g, valid_ref[g].astype(jnp.float32), flag)
    fa = lax.rsqrt(pa + level)
    fb = lax.rsqrt(pb + level)
    fe = lax.rsqrt(pe + level)
    factor = jnp.concatenate([fa, fa, fb, fb, fe], axis=1)
    whitened = (spec * factor * flag).astype(jnp.bfloat16)
    for b in range(8):
        white[b] = whitened[8 * b : 8 * b + 8]

    pl.semaphore_wait(barrier, jnp.where(own, 30, 31))

    l1 = []
    for d in (2, 6, 1, 3, 5, 7, 4):
        other = lax.rem(m + d, 8)
        cp = pltpu.make_async_remote_copy(
            src_ref=white.at[other], dst_ref=c1.at[m],
            send_sem=l1_send.at[d], recv_sem=l1_recv.at[d],
            device_id=(other * 8 + w, S), device_id_type=MESH,
        )
        cp.start()
        l1.append(cp)
    c1[m] = white[m]

    rc = []
    for d in range(1, 8):
        cp = pltpu.make_async_remote_copy(
            src_ref=white, dst_ref=rcv.at[S],
            send_sem=rc_send.at[d], recv_sem=rc_recv.at[d],
            device_id=(R, lax.rem(S + d, 8)), device_id_type=MESH,
        )
        cp.start()
        rc.append(cp)
    rcv[S] = white[...]

    for cp in l1:
        cp.wait_recv()
    v = lax.broadcasted_iota(jnp.int32, (8, 1), 0) + 8 * (m % 2)
    cand = [c1[mm].astype(jnp.float32) for mm in range(8)]
    for p in range(PANELS):
        st = start_ref[p]
        pick = jnp.zeros((8, C), jnp.float32)
        for mm in range(8):
            j = 128 * mm + 16 * w + v - st
            pick = jnp.where((j >= 0) & (j < SRC), cand[mm], pick)
        p1[p] = pick.astype(jnp.bfloat16)

    l2 = []
    for d in range(8):
        to = S ^ d
        cp = pltpu.make_async_remote_copy(
            src_ref=p1, dst_ref=c2.at[w],
            send_sem=l2_send.at[d], recv_sem=l2_recv.at[w],
            device_id=(m * 8 + d, to), device_id_type=MESH,
        )
        l2.append(cp)
        if d == 0:
            pl.when(jnp.logical_not(own))(cp.start)
        else:
            cp.start()

    @pl.when(own)
    def _():
        c2[w] = p1[...]

    for ww in range(8):
        cp = pltpu.make_async_remote_copy(
            src_ref=p1, dst_ref=c2.at[ww],
            send_sem=l2_send.at[0], recv_sem=l2_recv.at[ww],
            device_id=(m * 8, S), device_id_type=MESH,
        )
        if ww == 0:
            pl.when(jnp.logical_not(own))(cp.wait_recv)
        else:
            cp.wait_recv()

    for p in range(PANELS):
        st = start_ref[p]
        pick = jnp.zeros((8, C), jnp.float32)
        for ww in range(8):
            j = (16 * ww + v - st) & (SRC - 1)
            pick = jnp.where((j >> 4) == S, c2[ww, p].astype(jnp.float32), pick)
        src[yl, core, zr, zq, p] = pick.astype(jnp.bfloat16)

    near = zq // 2
    far = 1 - near
    g1 = {}
    for x in (2, 1, 3):
        piece = src.at[yl, core, zr, zq]
        g1[x] = pltpu.make_async_remote_copy(
            src_ref=piece, dst_ref=piece,
            send_sem=g1_send.at[x], recv_sem=g1_recv.at[x],
            device_id=(dev(yl, (zq ^ x) * 4 + zr, core), S), device_id_type=MESH,
        )
        g1[x].start()

    def group(i):
        k = i // 2
        return yl ^ (i % 2), lax.rem(zr + (k ^ (k // 2)), 4)

    def pair(i, half, c):
        y, q = group(i)
        return src.at[y, c, q, pl.ds(2 * half, 2)]

    def window(i, half, ref):
        dz, dy = (i // 2) ^ (i // 4), i % 2
        to = (0, -1, 2 - 4 * half, 1)[dz]
        return pltpu.make_async_remote_copy(
            src_ref=ref, dst_ref=ref,
            send_sem=g2_send.at[i, half], recv_sem=g2_recv.at[i, half],
            device_id=(dev(yl ^ dy, along(to), core), S), device_id_type=MESH,
        )

    def across(i, half):
        return pltpu.make_async_remote_copy(
            src_ref=pair(i, half, core), dst_ref=pair(i, half, core),
            send_sem=sib_send.at[i, half], recv_sem=sib_recv.at[i, half],
            device_id=(sibling, S), device_id_type=MESH,
        )

    for i in range(1, 8):
        window(i, near, src.at[yl, core, zr, zq]).start()
    g1[1].wait_recv()
    for i in range(1, 8):
        window(i, near, src.at[yl, core, zr, zq ^ 1]).start()
    across(0, near).start()
    for x in (3, 2):
        g1[x].wait_recv()
        for i in range(1, 8):
            window(i, far, src.at[yl, core, zr, zq ^ x]).start()
    across(0, far).start()

    for cp in rc:
        cp.wait_recv()

    def widen(sp, carry):
        for b in range(8):
            block = rcv[sp, b].astype(jnp.float32)
            rcvf[sp * 4 + b // 2, b % 2, :, pl.ds(0, C)] = block
            rcvf[sp * 4 + b // 2, b % 2, :, pl.ds(C, 128)] = pltpu.roll(
                block[:, 512:640], 64, 1
            )
        return carry

    lax.fori_loop(0, 8, widen, 0)

    def chunk(*parts):
        segs = []
        for g, (i, half, c) in enumerate(parts):
            y, q = group(i)
            segs.append(4 * ((q * 2 + c) ^ S) + 2 * y + half)
            for n in range(2):
                for p in range(PANELS):
                    srcf[2 * g + n, p] = src[y, c, q, 2 * half + n, p].astype(
                        jnp.float32
                    )

        def panel(p, carry):
            for vg in range(4):
                for t in range(3):
                    lanes = [pl.ds(256 * t, 128), pl.ds(256 * t + 128, 128)]
                    sums = [
                        [
                            [acc[p, vg * 4 + i, half, :, ln] for ln in lanes]
                            for half in range(2)
                        ]
                        for i in range(4)
                    ]
                    for g in range(2):
                        n = 2 * g + vg // 2
                        got = [
                            [rcvf[segs[g], half, :, ln] for ln in lanes]
                            for half in range(2)
                        ]
                        for i in range(4):
                            row = pl.ds((vg % 2) * 4 + i, 1)
                            s0 = srcf[n, p, row, lanes[0]]
                            if t < 2:
                                s1 = srcf[n, p, row, lanes[1]]
                            for half in range(2):
                                r0, r1 = got[half]
                                here = sums[i][half]
                                if t < 2:
                                    here[0] = here[0] + s0 * r0 + s1 * r1
                                    here[1] = here[1] + s0 * r1 - s1 * r0
                                else:
                                    here[0] = here[0] + s0 * r0
                                    here[1] = here[1] + s0 * r1
                    for i in range(4):
                        for half in range(2):
                            for n in range(2):
                                acc[p, vg * 4 + i, half, :, lanes[n]] = sums[i][half][n]
            return carry

        lax.fori_loop(0, PANELS, panel, 0)

    def half_of(j):
        return jnp.where(j < 8, near, far)

    def arrived(i, half):
        ref = pair(0, near, core)
        return pltpu.make_async_remote_copy(
            src_ref=ref, dst_ref=ref,
            send_sem=g2_send.at[i, half], recv_sem=g2_recv.at[i, half],
            device_id=(sibling, S), device_id_type=MESH,
        )

    def take(j):
        i, half = j % 8, half_of(j)

        @pl.when(i > 0)
        def _():
            arrived(i, half).wait_recv()
            across(i, half).start()

        return i, half, core

    def given(j):
        i, half = j % 8, half_of(j)
        across(i, half).wait_recv()
        return i, half, 1 - core

    def first(t, carry):
        chunk(take(2 * t), take(2 * t + 1))
        return carry

    def middle(j, carry):
        chunk(take(j), given(j - 4))
        return carry

    def final(t, carry):
        chunk(given(2 * t), given(2 * t + 1))
        return carry

    lax.fori_loop(0, 2, first, 0)
    lax.fori_loop(4, 16, middle, 0)
    lax.fori_loop(6, 8, final, 0)

    inv_copy.wait()
    for p in range(PANELS):
        st = start_ref[p]
        for i in range(16):
            xb[pl.ds(16 * i, 16)] = (
                acc[p, (st + i) & 15].reshape(16, W).astype(jnp.bfloat16)
            )
        out_ref[p] = jnp.dot(
            xb[...], inv[...], preferred_element_type=jnp.float32
        )

    for cp in l1 + rc + [g1[1], g1[2], g1[3]] + l2[1:]:
        cp.wait_send()
    pl.when(jnp.logical_not(own))(l2[0].wait_send)

    def drain(j, carry):
        i, half = j % 8, half_of(j)
        across(i, half).wait_send()

        @pl.when(i > 0)
        def _():
            arrived(i, half).wait_send()

        return carry

    lax.fori_loop(0, 16, drain, 0)


def body(traces, panel_start, valid):
    rows, segs, samples = traces.shape
    tables = np.zeros((KPAD + W, C), ml_dtypes.bfloat16)
    tables[:KPAD] = forward_table(samples)
    tables[KPAD:, : 2 * LAG] = inverse_table()
    bf = jnp.bfloat16
    f32 = jnp.float32
    dma = pltpu.SemaphoreType.DMA
    out = pl.pallas_call(
        kernel,
        out_shape=jax.ShapeDtypeStruct((PANELS, 256, 2 * LAG), f32),
        in_specs=[
            pl.BlockSpec(memory_space=pltpu.SMEM),
            pl.BlockSpec(memory_space=pltpu.SMEM),
            pl.BlockSpec(memory_space=pl.ANY),
            pl.BlockSpec(memory_space=pl.ANY),
        ],
        out_specs=pl.BlockSpec(memory_space=pltpu.VMEM),
        scratch_shapes=[
            pltpu.VMEM((rows, segs, samples), bf),
            pltpu.VMEM((KPAD, C), bf),
            pltpu.VMEM((W, 2 * LAG), bf),
            pltpu.VMEM((8, 8, C), bf),
            pltpu.VMEM((8, 8, C), bf),
            pltpu.VMEM((2, 8, C), bf),
            pltpu.VMEM((8, 2, 8, C), bf),
            pltpu.VMEM((2, 2, 4, 4, 2, 8, C), bf),
            pltpu.VMEM((8, 8, 8, C), bf),
            pltpu.VMEM((SEGS, 2, 8, W), f32),
            pltpu.VMEM((4, 2, 8, C), f32),
            pltpu.VMEM((2, 16, 2, 8, W), f32),
            pltpu.VMEM((256, W), bf),
            dma((5,)),
            dma((8,)), dma((8,)), dma((8,)), dma((8,)), dma((8,)), dma((8,)),
            dma((4,)), dma((4,)), dma((8, 2)), dma((8, 2)), dma((8, 2)), dma((8, 2)),
        ],
        compiler_params=pltpu.CompilerParams(
            collective_id=0, has_side_effects=True, vmem_limit_bytes=62 * 1024 * 1024
        ),
    )(panel_start, valid, traces, jnp.asarray(tables))
    total_segs = segs * lax.axis_size("seg")
    out = out * (1.0 / math.sqrt(F * total_segs))
    return out.reshape(PANELS, 16, 16, 2 * LAG)


def solution(mesh):
    return jax.shard_map(
        body,
        mesh=mesh,
        in_specs=(P("rcv", "seg", None), P(), P("seg")),
        out_specs=P(None, "seg", "rcv", None),
        check_vma=False,
    )
```
